128 devices in a mesh: blk: 16 (over x_hi, y, core), pool: 8 (over z, x_lo).
Axes of the slice: x: 4 (x_hi: 2, x_lo: 2; x = x_hi * 2 + x_lo), y: 4, z: 4, core: 2. Of those that a mesh axis runs over, the one named last changes fastest.
Arguments:
- pre_q: bfloat16 [16384, 4096], P('blk', 'pool'), may hold values from -6 to 6
- pre_k: bfloat16 [16384, 512], P('blk', 'pool'), may hold values from -6 to 6
- pre_v: bfloat16 [16384, 512], P('blk', 'pool'), may hold values from -6 to 6
- routes: int32 [1024, 1], P('blk'), may hold values from 0 to 7; in each aligned block of 64 rows (0 to 63, 64 to 127, ...) at most 16 rows name the same one
- dec_q: bfloat16 [512, 4, 4096], P(('blk', 'pool')), may hold values from -6 to 6
- dec_k: bfloat16 [512, 4, 512], P(('blk', 'pool')), may hold values from -6 to 6
- dec_v: bfloat16 [512, 4, 512], P(('blk', 'pool')), may hold values from -6 to 6
- table: int32 [512, 8], P(('blk', 'pool')), may hold values from 0 to 15
- ctx_len: int32 [512], P(('blk', 'pool')), may hold values from 1 to 128, as said below
Outputs:
- pre_out: bfloat16 [16384, 4096], P('blk', 'pool')
- dec_out: bfloat16 [512, 4, 4096], P(('blk', 'pool'))
The draws below stay inside these ranges and needn't reach their ends.
Inputs may be any that keep to these rules, and one draw needn't show every extreme that they name: `routes`: among the 64 pages of one block at most 16 go to one pool index; some pool index takes exactly 16. `ctx_len`: some row has exactly 128.
All inputs are finite; a program needn't handle non-finite values.
Results may differ from the reference program's by a relative error of at most 0.0065.
Values may be sent and summed in bfloat16 or wider, within the bound.
A program may use at most 64 MiB of HBM per device.

```python
import math
import jax
import jax.numpy as jnp
import numpy as np
from jax import lax

HQ = 32
KVH = 4
DH = 128
PAGE = 16
STEPS = 4
DROW_DEV = 4
PPR = 8
SEQ_LEN = 16384
PAGES_DEV = 64
CAP = 16
DROWS = 512
N_BLK = 16
N_POOL = 8


def draw_pre_q(key, part):
    key = jax.random.fold_in(key, 11)
    array_shape = (SEQ_LEN, HQ * DH)
    values = jnp.clip(jax.random.normal(key, array_shape, jnp.float32), -6.0, 6.0)
    return values.astype(jnp.bfloat16)


def draw_pre_k(key, part):
    key = jax.random.fold_in(key, 12)
    array_shape = (SEQ_LEN, KVH * DH)
    values = jnp.clip(jax.random.normal(key, array_shape, jnp.float32), -6.0, 6.0)
    return values.astype(jnp.bfloat16)


def draw_dec_q(key, part):
    key = jax.random.fold_in(key, 13)
    array_shape = (DROWS, STEPS, HQ * DH)
    values = jnp.clip(jax.random.normal(key, array_shape, jnp.float32), -6.0, 6.0)
    return values.astype(jnp.bfloat16)


def draw_dec_k(key, part):
    key = jax.random.fold_in(key, 14)
    array_shape = (DROWS, STEPS, KVH * DH)
    values = jnp.clip(jax.random.normal(key, array_shape, jnp.float32), -6.0, 6.0)
    return values.astype(jnp.bfloat16)


def draw_ctx_len(key, part):
    key = jax.random.fold_in(key, 15)
    first_key, second_key = jax.random.split(key)
    lengths = jax.random.randint(first_key, (DROWS,), 1, PPR * PAGE + 1, jnp.int32)
    chosen = jax.random.randint(second_key, (), 0, DROWS, jnp.int32)
    return lengths.at[chosen].set(PPR * PAGE)


def plant(drawn, rng, smallest, largest):
    index_at = [jax.random.randint(jax.random.fold_in(rng, axis), (), 0, length) for axis, length in enumerate(drawn.shape)]
    widest = drawn.shape.index(max(drawn.shape))
    next_to = index_at[:widest] + [(index_at[widest] + 1) % drawn.shape[widest]] + index_at[widest + 1:]
    return drawn.at[tuple(index_at)].set(smallest).at[tuple(next_to)].set(largest)


def block_scale(stream_key, dims, cuts, smallest, high):
    def one(dim, shards_of):
        draws = jax.random.uniform(jax.random.fold_in(jax.random.fold_in(stream_key, 6), dim), (shards_of,), jnp.float32, smallest / len(cuts), high / len(cuts))
        return jnp.repeat(jnp.exp(draws), dims[dim] // shards_of).reshape((-1,) + (1,) * (len(dims) - dim - 1))

    loudness = one(*cuts[0])
    for cut in cuts[1:]:
        loudness = loudness * one(*cut)
    return loudness


def routed_block(stream_key, own, number, rows, number_of, top, bound, skew):
    order = jax.random.permutation(stream_key, number_of)
    crowded, ordinary = shares(number_of, rows * top, bound, skew, True), shares(number_of, rows * top, bound, skew, False)
    places = jnp.arange(number_of)

    def named(sizes, rotation):
        used = int((sizes > 0).sum())
        fixed = max(1, used // 4)
        passed = fixed + (places - fixed + rotation * (used - fixed)) % max(1, number_of - fixed)
        return jnp.zeros((number_of,), jnp.int32).at[order[jnp.where(places < fixed, places, passed)]].set(jnp.asarray(sizes, jnp.int32))

    sizes = jnp.where(number % 4 == 0, named(crowded, number // 4), named(ordinary, number - number // 4 - 1))
    mixed = jax.random.permutation(jax.random.fold_in(own, 3), number_of)
    giver, taker = mixed[0:number_of // 2 * 2:2], mixed[1:number_of // 2 * 2:2]
    room = jnp.minimum(sizes[giver] - 1, bound - sizes[taker]) // 2
    room = jnp.where((giver == order[0]) | (taker == order[0]) | (sizes[taker] == 0), 0, jnp.maximum(room, 0))
    passed = jax.random.randint(jax.random.fold_in(own, 4), (number_of // 2,), 0, 1 << 20) % (room + 1)
    sizes = sizes.at[giver].add(-passed).at[taker].add(passed)
    members = jnp.searchsorted(jnp.cumsum(sizes), jnp.arange(rows * top), side="right").astype(jnp.int32)
    table = members.reshape(top, rows).T
    table = table[jax.random.permutation(jax.random.fold_in(own, 1), rows)]
    rotation = jax.random.randint(jax.random.fold_in(own, 2), (rows, 1), 0, top)
    return jnp.take_along_axis(table, (jnp.arange(top)[None, :] + rotation) % top, axis=1)


def shares(number_of, total, limit, skew, full):
    portions = [(1 << 20) // math.isqrt(standing ** skew) + 1 for standing in range(1, number_of + 1)]
    largest = limit if full else min(limit, max(-(-total // number_of), total * portions[0] // sum(portions)))
    least = 1 if total - largest >= number_of - 1 else 0
    given, spare = [largest] + [least] * (number_of - 1), total - largest - least * (number_of - 1)
    while spare > 0:
        candidates = [i for i in range(1, number_of) if given[i] < largest] or [i for i in range(1, number_of) if given[i] < limit]
        mass, budget = sum([portions[i] for i in candidates]), spare
        for i in candidates:
            more = min(limit - given[i], max(1, budget * portions[i] // mass), spare)
            given[i] = given[i] + more
            spare = spare - more
    return np.array(given)


def normal_values(key, extent, deviation, bound, cuts=(), kind=jnp.bfloat16):
    array = jax.random.normal(key, extent, jnp.float32) * deviation
    if len(cuts) > 0:
        array = block_scale(key, extent, cuts, -0.22, 0.18) * array
    return jnp.clip(array, min=-bound, max=bound).astype(kind)


def setup_inputs(seed: int = 0) -> dict:
    seeds = jax.random.split(jax.random.key(seed), 10)
    pre_q = draw_pre_q(jax.random.fold_in(seeds[9], 71), 0)
    pre_k = draw_pre_k(jax.random.fold_in(seeds[9], 71), 0)
    pre_v = normal_values(seeds[2], (SEQ_LEN, KVH * DH), 1.0, 6.0, ((0, 16), (1, 8)))
    routes_keys = jax.random.split(jax.random.fold_in(seeds[3], 1), (PAGES_DEV * N_BLK) // PAGES_DEV)
    routes_turns = jax.random.permutation(jax.random.fold_in(seeds[3], 3), (PAGES_DEV * N_BLK) // PAGES_DEV)
    routes = jax.vmap(lambda own, number: routed_block(jax.random.fold_in(seeds[3], 2), own, number, PAGES_DEV, N_POOL, 1, CAP, 2))(routes_keys, routes_turns).reshape((PAGES_DEV * N_BLK, 1))
    dec_q = draw_dec_q(jax.random.fold_in(seeds[9], 71), 0)
    dec_k = draw_dec_k(jax.random.fold_in(seeds[9], 71), 0)
    dec_v = normal_values(seeds[6], (DROWS, STEPS, KVH * DH), 1.0, 6.0, ((0, 128),))
    table = plant(jax.random.randint(seeds[7], (DROWS, PPR), 0, CAP), jax.random.fold_in(seeds[7], 1), 0, CAP - 1).astype(jnp.int32)
    ctx_len = draw_ctx_len(jax.random.fold_in(seeds[9], 71), 0)
    return {"pre_q": pre_q, "pre_k": pre_k, "pre_v": pre_v, "routes": routes, "dec_q": dec_q, "dec_k": dec_k, "dec_v": dec_v, "table": table, "ctx_len": ctx_len}


NEG = -1.0e30


def prefill_one(queries, key_rows, value_rows):
    group_size = HQ // KVH
    block = math.gcd(SEQ_LEN, 256)
    key_float = key_rows.astype(jnp.float32).reshape(SEQ_LEN, KVH, DH)
    value_float = value_rows.astype(jnp.float32).reshape(SEQ_LEN, KVH, DH)
    key_positions = jnp.arange(SEQ_LEN, dtype=jnp.int32)
    query_blocks = queries.reshape(SEQ_LEN // block, block, KVH, group_size, DH)
    starts = jnp.arange(SEQ_LEN // block, dtype=jnp.int32) * block

    def one_block(packed):
        rows_in, row_first = packed
        scores = jnp.einsum('tkgd,skd->kgts', rows_in.astype(jnp.float32), key_float) * DH ** -0.5
        query_positions = row_first + jnp.arange(block, dtype=jnp.int32)
        visible = query_positions[:, None] >= key_positions[None, :]
        scores = jnp.where(visible, scores, NEG)
        row_max = jnp.max(scores, axis=-1, keepdims=True)
        weights = jnp.where(visible, jnp.exp(scores - row_max), 0.0)
        row_sum = jnp.sum(weights, axis=-1)
        rounded = lax.optimization_barrier(weights.astype(jnp.bfloat16)).astype(jnp.float32)
        blended = jnp.einsum('kgts,skd->tkgd', rounded, value_float)
        blended = blended / jnp.transpose(row_sum, (2, 0, 1))[..., None]
        return blended.astype(jnp.bfloat16).reshape(block, HQ * DH)

    return lax.map(one_block, (query_blocks, starts)).reshape(SEQ_LEN, HQ * DH)


def decode_device(page_store, queries, new_keys, new_values, slot_table, lengths):
    group_size = HQ // KVH
    row_count = queries.shape[0]
    picked = page_store[slot_table].reshape(row_count, PPR * PAGE, 2, KVH, DH).astype(jnp.float32)
    cache_keys = picked[:, :, 0]
    cache_values = picked[:, :, 1]
    query_float = queries.astype(jnp.float32).reshape(row_count, STEPS, KVH, group_size, DH)
    fresh_keys = new_keys.astype(jnp.float32).reshape(row_count, STEPS, KVH, DH)
    fresh_values = new_values.astype(jnp.float32).reshape(row_count, STEPS, KVH, DH)
    score_cache = jnp.einsum('rtkgd,rskd->rkgts', query_float, cache_keys) * DH ** -0.5
    score_fresh = jnp.einsum('rtkgd,rukd->rkgtu', query_float, fresh_keys) * DH ** -0.5
    live_cache = (jnp.arange(PPR * PAGE, dtype=jnp.int32)[None, :] < lengths[:, None])[:, None, None, None, :]
    live_fresh = jnp.arange(STEPS, dtype=jnp.int32)[:, None] >= jnp.arange(STEPS, dtype=jnp.int32)[None, :]
    score_cache = jnp.where(live_cache, score_cache, NEG)
    score_fresh = jnp.where(live_fresh, score_fresh, NEG)
    row_max = jnp.maximum(jnp.max(score_cache, axis=-1), jnp.max(score_fresh, axis=-1))[..., None]
    weight_cache = jnp.where(live_cache, jnp.exp(score_cache - row_max), 0.0)
    weight_fresh = jnp.where(live_fresh, jnp.exp(score_fresh - row_max), 0.0)
    row_sum = jnp.sum(weight_cache, axis=-1) + jnp.sum(weight_fresh, axis=-1)
    round_cache = lax.optimization_barrier(weight_cache.astype(jnp.bfloat16)).astype(jnp.float32)
    round_fresh = lax.optimization_barrier(weight_fresh.astype(jnp.bfloat16)).astype(jnp.float32)
    blended = jnp.einsum('rkgts,rskd->rtkgd', round_cache, cache_values)
    blended = blended + jnp.einsum('rkgtu,rukd->rtkgd', round_fresh, fresh_values)
    blended = blended / jnp.transpose(row_sum, (0, 3, 1, 2))[..., None]
    return blended.astype(jnp.bfloat16).reshape(row_count, STEPS, HQ * DH)


def reference(pre_q, pre_k, pre_v, routes, dec_q, dec_k, dec_v, table, ctx_len):
    pre_out = prefill_one(pre_q, pre_k, pre_v)
    stacked = jnp.stack([pre_k, pre_v], axis=1)
    pages = stacked.reshape(N_BLK, PAGES_DEV, PAGE, 2, KVH * DH)
    owner_pool = routes[:, 0].reshape(N_BLK, PAGES_DEV)
    onehot = (owner_pool[..., None] == jnp.arange(N_POOL, dtype=jnp.int32)).astype(jnp.int32)
    page_rank = jnp.sum((jnp.cumsum(onehot, axis=1) - onehot) * onehot, axis=-1).astype(jnp.int32)
    blk_index = jnp.broadcast_to(jnp.arange(N_BLK, dtype=jnp.int32)[:, None], owner_pool.shape)
    page_store = jnp.zeros((N_BLK, N_POOL, CAP, PAGE, 2, KVH * DH), jnp.bfloat16)
    page_store = page_store.at[blk_index, owner_pool, page_rank].set(pages)
    page_store = page_store.reshape(N_BLK * N_POOL, CAP, PAGE, 2, KVH * DH)
    devices = N_BLK * N_POOL
    dec_out = jax.vmap(decode_device)(
        page_store,
        dec_q.reshape(devices, DROW_DEV, STEPS, HQ * DH),
        dec_k.reshape(devices, DROW_DEV, STEPS, KVH * DH),
        dec_v.reshape(devices, DROW_DEV, STEPS, KVH * DH),
        table.reshape(devices, DROW_DEV, PPR),
        ctx_len.reshape(devices, DROW_DEV))
    return pre_out, dec_out.reshape(DROWS, STEPS, HQ * DH)
```

```python
import functools

import jax
import jax.numpy as jnp
from jax import lax
from jax.experimental import pallas as pl
from jax.experimental.pallas import tpu as pltpu
from jax.sharding import PartitionSpec as P

HQ = 32
KVH = 4
DH = 128
PAGE = 16
STEPS = 4
PPR = 8
CAP = 16

N_BLK = 16
N_POOL = 8
ROWS = 1024
HALF = ROWS // 2
TILE = 512
TILES = 8
GUESTS = 4
SCALE2 = DH**-0.5 * 1.4426950408889634
SAFE = 100.0
NEG = -1e30
MESH = pl.DeviceIdType.MESH

A1, A2, B1, B2, SIB, COPIES = 0, 2, 4, 12, 20, 36


def fused_kernel(q_ref, kp_ref, vt_ref, psend_ref,
                 out_ref, precv_ref, kall_ref, vall_ref, bound_ref,
                 kbuf, vbuf, qst, qz, acc, ostage, kmx,
                 send, recv, qsend, qrecv, osend, orecv, psend_sem, precv_sem, local):
    blk, pool = lax.axis_index("blk"), lax.axis_index("pool")
    core = lax.rem(blk, 2)
    cb = blk // 2
    x_hi, y = cb // 4, lax.rem(cb, 4)
    z, x_lo = pool // 2, lax.rem(pool, 2)
    mirror = N_BLK - 1 - blk

    def block_of(xh, yy):
        return (xh * 4 + yy) * 2 + core

    def along_x(k):
        return ((x_hi, x_lo), (x_hi, 1 - x_lo), (1 - x_hi, 1 - x_lo), (1 - x_hi, x_lo))[k]

    def along_y(k):
        return lax.rem(y + (0, 1, 3, 2)[k], 4)

    def device(kx, ky):
        xh, xl = along_x(kx)
        return (block_of(xh, along_y(ky)), z * 2 + xl)

    sibling = (blk + 1 - 2 * core, pool)

    barrier = pltpu.get_barrier_semaphore()
    peers = [device(2, 0), device(0, 1), device(0, 2), sibling, (mirror, pool)]
    peers += [(blk, lax.rem(pool + d, N_POOL)) for d in range(1, N_POOL)]
    for peer in peers:
        pl.semaphore_signal(barrier, inc=1, device_id=peer, device_id_type=MESH)

    kbuf[blk, x_lo] = kp_ref[...]
    vbuf[blk, x_lo] = vt_ref[...]
    for u in range(TILES):
        t, hp = u // 2, u % 2
        for h in range(2):
            col = (hp * 2 + h) * DH
            qst[u, h * 256:(h + 1) * 256, :] = q_ref[t * 256:(t + 1) * 256, col:col + DH]
    pl.semaphore_wait(barrier, len(peers))

    class Gather:
        def __init__(self, index, buf, rows, x_first):
            self.index, self.buf, self.rows, self.x_first = index, buf, rows, x_first

        def place(self, ka, kb):
            return (ka, kb) if self.x_first else (kb, ka)

        def piece(self, ka, kb, half=None):
            kx, ky = self.place(ka, kb)
            xh, xl = along_x(kx)
            whole = self.buf.at[block_of(xh, along_y(ky)), xl]
            if half is None:
                return whole
            return whole.at[pl.ds(half * self.rows // 2, self.rows // 2)]

        def copy(self, slot, ka, kb, half, to, there=None):
            there = slot if there is None else there
            ref = self.piece(ka, kb, half)
            return pltpu.make_async_remote_copy(
                src_ref=ref, dst_ref=ref,
                send_sem=send.at[self.index, slot], recv_sem=recv.at[self.index, there],
                device_id=to, device_id_type=MESH)

        def neighbour(self, axis, n):
            ka, kb = ((n + 1, 0), (0, n + 1))[axis]
            return device(*self.place(ka, kb))

        def seen(self, axis, n):
            is_x = (axis == 0) == self.x_first
            return n if is_x else 1 - n

        def all_copies(self):
            out = {}
            for n in range(2):
                out["a1", n] = lambda n=n: self.copy(
                    A1 + n, 0, 0, None, self.neighbour(0, n), A1 + self.seen(0, n))
                out["a2", n] = lambda n=n: self.copy(
                    A2 + n, 2 - n, 0, n, self.neighbour(0, n))
                for ka in range(4):
                    out["b1", ka, n] = lambda n=n, ka=ka: self.copy(
                        B1 + ka * 2 + n, ka, 0, None, self.neighbour(1, n),
                        B1 + ka * 2 + self.seen(1, n))
                    out["b2", ka, n] = lambda n=n, ka=ka: self.copy(
                        B2 + ka * 2 + n, ka, 2 - n, n, self.neighbour(1, n))
            for ka in range(4):
                for kb in range(4):
                    out["sib", ka, kb] = lambda ka=ka, kb=kb: self.copy(
                        SIB + ka * 4 + kb, ka, kb, None, sibling)
            return out

        def start(self, *key):
            self.all_copies()[key]().start()

        def arrive(self, slot, ka, kb, half=None):
            ref = self.piece(ka, kb, half)
            pltpu.make_async_remote_copy(
                src_ref=ref, dst_ref=ref, send_sem=send.at[self.index, slot],
                recv_sem=recv.at[self.index, slot], device_id=sibling,
                device_id_type=MESH).wait_recv()

        def got_a1(self, n):
            self.arrive(A1 + n, n + 1, 0)
            self.start("a2", 1 - n)
            self.start("sib", n + 1, 0)
            self.start("b1", n + 1, 0)
            self.start("b1", n + 1, 1)

        def got_a2(self):
            for half in range(2):
                self.arrive(A2 + half, 3, 0, half)
            self.start("sib", 3, 0)
            self.start("b1", 3, 0)
            self.start("b1", 3, 1)

        def got_b1(self, ka, n):
            self.arrive(B1 + ka * 2 + n, ka, n + 1)
            self.start("b2", ka, 1 - n)
            self.start("sib", ka, n + 1)

        def got_b2(self, ka):
            for half in range(2):
                self.arrive(B2 + ka * 2 + half, ka, 3, half)
            self.start("sib", ka, 3)

        def got_sib(self, ka, kb):
            kx, ky = self.place(ka, kb)
            xh, xl = along_x(kx)
            there = (xh * 4 + along_y(ky)) * 2 + 1 - core
            ref = self.buf.at[there, xl]
            slot = SIB + ka * 4 + kb
            pltpu.make_async_remote_copy(
                src_ref=ref, dst_ref=ref, send_sem=send.at[self.index, slot],
                recv_sem=recv.at[self.index, slot], device_id=sibling,
                device_id_type=MESH).wait_recv()

        def sib_xy(self, kx, ky):
            self.got_sib(*((kx, ky) if self.x_first else (ky, kx)))

        def finish(self):
            for make in self.all_copies().values():
                make().wait_send()

    keys = Gather(0, kbuf, HALF, True)
    values = Gather(1, vbuf, DH // 2, False)

    keys.start("a1", 0)
    values.start("b1", 0, 0)
    keys.start("sib", 0, 0)
    values.start("sib", 0, 0)
    keys.start("a1", 1)
    values.start("b1", 0, 1)
    for n in range(2):
        values.start("a1", n)
        keys.start("b1", 0, n)

    high = blk >= N_BLK // 2
    moved = jnp.where(high, y + 1, 4 - y)
    mine = jnp.where(high, TILES - moved, TILES)
    guests = jnp.where(high, 0, moved)

    def q_copy(v):
        return pltpu.make_async_remote_copy(
            src_ref=qst.at[TILES - 1 - v], dst_ref=qst.at[TILES + v],
            send_sem=qsend.at[v], recv_sem=qrecv.at[v],
            device_id=(mirror, pool), device_id_type=MESH)

    def o_copy(v):
        return pltpu.make_async_remote_copy(
            src_ref=ostage.at[TILES + v], dst_ref=out_ref.at[TILES - 1 - v],
            send_sem=osend.at[v], recv_sem=orecv.at[v],
            device_id=(mirror, pool), device_id_type=MESH)

    def when_loop(count, body):
        def step(v, carry):
            body(v)
            return carry
        lax.fori_loop(0, count, step, 0)

    sent_tiles = jnp.where(high, moved, 0)
    when_loop(sent_tiles, lambda v: q_copy(v).start())

    def page_copy(d):
        to = lax.rem(pool + d, N_POOL)
        return pltpu.make_async_remote_copy(
            src_ref=psend_ref.at[to], dst_ref=precv_ref.at[pool],
            send_sem=psend_sem.at[d], recv_sem=precv_sem.at[d],
            device_id=(blk, to), device_id_type=MESH)

    def page_arrive(d):
        origin = lax.rem(pool + N_POOL - d, N_POOL)
        ref = precv_ref.at[origin]
        pltpu.make_async_remote_copy(
            src_ref=ref, dst_ref=ref, send_sem=psend_sem.at[d], recv_sem=precv_sem.at[d],
            device_id=sibling, device_id_type=MESH).wait_recv()

    own_pages = pltpu.make_async_copy(psend_ref.at[pool], precv_ref.at[pool], local.at[0])

    d_in = lax.broadcasted_iota(jnp.int32, (DH, 4 * DH), 0)
    column = lax.broadcasted_iota(jnp.int32, (DH, 4 * DH), 1)
    half, lane = column // 256, lax.rem(column, 256)
    source = lax.rem(lane, 128) - 64 * half
    spread = jnp.where((source >= 0) & (source < 64) & (source + (lane // 128) * 64 == d_in),
                       1.0, 0.0).astype(jnp.bfloat16)

    def pad_queries(u):
        wide = jnp.dot(qst[u], spread, preferred_element_type=jnp.float32).astype(jnp.bfloat16)
        qz[u, 0] = wide[:, :256]
        qz[u, 1] = wide[:, 256:]
        acc[u] = jnp.zeros((144, TILE), jnp.float32)

    when_loop(mine, pad_queries)
    kmx[...] = jnp.zeros_like(kmx)

    ones = jnp.ones((16, HALF), jnp.bfloat16)

    def scores(u, block, h):
        keys_in = jnp.concatenate([kbuf[block, 0], kbuf[block, 1]], axis=1)
        return lax.dot_general(keys_in, qz[u, h], (((1,), (1,)), ((), ())),
                               preferred_element_type=jnp.float32)

    def mixed(s, block, h, visible=None):
        weights = jnp.exp2(s * SCALE2)
        if visible is not None:
            weights = jnp.where(visible, weights, 0.0)
        cut = slice(h * HALF, (h + 1) * HALF)
        values_in = jnp.concatenate([vbuf[block, 0, :, cut], vbuf[block, 1, :, cut], ones], axis=0)
        return jnp.dot(values_in, weights.astype(jnp.bfloat16), preferred_element_type=jnp.float32)

    def full(u, chunks):
        ahead = scores(u, *chunks[0])
        total = None
        for i, chunk in enumerate(chunks):
            now = ahead
            if i + 1 < len(chunks):
                ahead = scores(u, *chunks[i + 1])
            part = mixed(now, *chunk)
            total = part if total is None else total + part
        acc[u] += total

    def diagonal(u, t, block):
        key_at = lax.broadcasted_iota(jnp.int32, (HALF, TILE), 0)
        row_at = lax.rem(lax.broadcasted_iota(jnp.int32, (HALF, TILE), 1), 256)
        late = t // 2
        visible = key_at <= row_at + (t - 2 * late) * 256

        @pl.when(late == 0)
        def _():
            acc[u] += mixed(scores(u, block, 0), block, 0, visible)

        @pl.when(late == 1)
        def _():
            first, second = scores(u, block, 0), scores(u, block, 1)
            acc[u] += mixed(first, block, 0) + mixed(second, block, 1, visible)

    def tile_turn(u, t, tile_block, at):
        tile_cb = tile_block // 2

        @pl.when(at < tile_cb)
        def _():
            full(u, [(2 * at, 0), (2 * at, 1), (2 * at + 1, 0), (2 * at + 1, 1)])

        @pl.when(at == tile_cb)
        def _():
            @pl.when(lax.rem(tile_block, 2) == 1)
            def _():
                full(u, [(2 * at, 0), (2 * at, 1)])
            diagonal(u, t, tile_block)

    def own_turn(at):
        @pl.when(at <= cb)
        def _():
            when_loop(mine, lambda u: tile_turn(u, u // 2, blk, at))

    def guest_turn(at):
        @pl.when(at <= mirror // 2)
        def _():
            when_loop(guests, lambda v: tile_turn(
                TILES + v, (TILES - 1 - v) // 2, mirror, at))

    def note_keys(at):
        for core_at in range(2):
            for xl in range(2):
                piece = jnp.abs(kbuf[2 * at + core_at, xl].astype(jnp.float32))
                kmx[xl] = jnp.maximum(kmx[xl], jnp.max(piece.reshape(HALF // 8, 8, DH), axis=0))
        for ref, buf, slot in ((kall_ref, kbuf, 0), (vall_ref, vbuf, 1)):
            pltpu.make_async_copy(buf.at[pl.ds(2 * at, 2)], ref.at[pl.ds(2 * at, 2)],
                                  local.at[1 + slot + 2 * at]).start()

    def keep_wait(at):
        for ref, buf, slot in ((kall_ref, kbuf, 0), (vall_ref, vbuf, 1)):
            pltpu.make_async_copy(buf.at[pl.ds(2 * at, 2)], ref.at[pl.ds(2 * at, 2)],
                                  local.at[1 + slot + 2 * at]).wait()

    def chip_block(kx, ky):
        return along_x(kx)[0] * 4 + along_y(ky)

    def whole(kx_pair, ky):
        for kx in kx_pair:
            keys.sib_xy(kx, ky)
            values.sib_xy(kx, ky)

    near, far = (0, 1), (2, 3)

    def turn(pair, ky):
        at = chip_block(pair[0], ky)
        whole(pair, ky)
        note_keys(at)
        guest_turn(at)
        own_turn(at)

    keys.got_a1(0)
    values.got_b1(0, 0)
    keys.got_a1(1)
    values.got_b1(0, 1)
    for n in range(2):
        values.got_a1(n)
        keys.got_b1(0, n)
    own_pages.start()
    for d in range(1, N_POOL):
        page_copy(d).start()

    def take_guest(v):
        q_copy(v).wait_recv()
        pad_queries(TILES + v)

    when_loop(guests, take_guest)
    turn(near, 0)
    keys.got_a2()
    values.got_a2()
    values.got_b2(0)
    turn(far, 0)
    for n in range(2):
        for ka in (1, 2):
            keys.got_b1(ka, n)
            values.got_b1(ka, n)
    turn(near, 1)
    for n in range(2):
        keys.got_b1(3, n)
        values.got_b1(3, n)
    keys.got_b2(0)
    turn(near, 2)
    values.got_b2(1)
    values.got_b2(2)
    turn(far, 1)
    keys.got_b2(1)
    keys.got_b2(2)
    turn(far, 2)
    keys.got_b2(3)
    values.got_b2(3)
    turn(near, 3)
    turn(far, 3)

    def result(u):
        total = acc[u]
        ostage[u] = (total[:DH] / total[DH:DH + 1]).T.astype(jnp.bfloat16)

    def send_back(v):
        result(TILES + v)
        o_copy(v).start()

    def own_out(u):
        return pltpu.make_async_copy(ostage.at[u], out_ref.at[u], local.at[17 + u])

    def keep(u):
        result(u)
        own_out(u).start()

    when_loop(guests, send_back)
    when_loop(mine, keep)

    kk = jnp.concatenate([jnp.max(kmx[0], axis=0, keepdims=True),
                          jnp.max(kmx[1], axis=0, keepdims=True)], axis=1)
    kk = jnp.broadcast_to(kk, (16, 256)).astype(jnp.bfloat16)
    bound_ref[...] = jnp.zeros_like(bound_ref)

    def reach(u):
        wide = jnp.abs(jnp.dot(qst[u], spread, preferred_element_type=jnp.float32)).astype(jnp.bfloat16)
        for h in range(2):
            far_score = lax.dot_general(kk, wide[:, h * 256:(h + 1) * 256],
                                        (((1,), (1,)), ((), ())),
                                        preferred_element_type=jnp.float32)
            bound_ref[...] = jnp.maximum(bound_ref[...], far_score)

    when_loop(TILES, reach)

    own_pages.wait()
    for d in range(1, N_POOL):
        page_arrive(d)
        page_copy(d).wait_send()
    when_loop(mine, lambda u: own_out(u).wait())
    when_loop(sent_tiles, lambda v: q_copy(v).wait_send())
    when_loop(guests, lambda v: o_copy(v).wait_send())
    when_loop(sent_tiles, lambda v: o_copy(v).wait_recv())
    keys.finish()
    values.finish()
    when_loop(N_BLK // 2, keep_wait)


def fused(q, kp, vt, psend):
    vmem = pl.BlockSpec(memory_space=pltpu.VMEM)
    anywhere = pl.BlockSpec(memory_space=pl.ANY)
    bf16, f32 = jnp.bfloat16, jnp.float32
    slots = TILES + GUESTS
    return pl.pallas_call(
        fused_kernel,
        out_shape=(
            jax.ShapeDtypeStruct((TILES, TILE, DH), bf16),
            jax.ShapeDtypeStruct((N_POOL, CAP * PAGE, DH), bf16),
            jax.ShapeDtypeStruct((N_BLK, 2, HALF, DH), bf16),
            jax.ShapeDtypeStruct((N_BLK, 2, DH // 2, ROWS), bf16),
            jax.ShapeDtypeStruct((16, TILE), f32),
        ),
        in_specs=[vmem, vmem, vmem, anywhere],
        out_specs=(anywhere, anywhere, anywhere, anywhere, vmem),
        scratch_shapes=[
            pltpu.VMEM((N_BLK, 2, HALF, DH), bf16),
            pltpu.VMEM((N_BLK, 2, DH // 2, ROWS), bf16),
            pltpu.VMEM((slots, TILE, DH), bf16),
            pltpu.VMEM((slots, 2, TILE, 256), bf16),
            pltpu.VMEM((slots, 144, TILE), f32),
            pltpu.VMEM((slots, TILE, DH), bf16),
            pltpu.VMEM((2, 8, DH), f32),
            pltpu.SemaphoreType.DMA((2, COPIES)),
            pltpu.SemaphoreType.DMA((2, COPIES)),
            pltpu.SemaphoreType.DMA((GUESTS,)),
            pltpu.SemaphoreType.DMA((GUESTS,)),
            pltpu.SemaphoreType.DMA((GUESTS,)),
            pltpu.SemaphoreType.DMA((GUESTS,)),
            pltpu.SemaphoreType.DMA((N_POOL,)),
            pltpu.SemaphoreType.DMA((N_POOL,)),
            pltpu.SemaphoreType.DMA((17 + TILES,)),
        ],
        compiler_params=pltpu.CompilerParams(
            collective_id=0, has_side_effects=True, vmem_limit_bytes=56 << 20),
        cost_estimate=pl.CostEstimate(flops=2 * 10**10, bytes_accessed=2 * 10**7,
                                      transcendentals=4 * 10**7),
        name="prefill",
    )(q, kp, vt, psend)


def online_attend(queries, first_row, key_rows, value_rows):
    count, length = queries.shape[0], key_rows.shape[0]
    per_head = queries.shape[1] // DH
    grouped = queries.reshape(count, per_head, DH)
    positions = first_row + jnp.arange(count, dtype=jnp.int32)
    step_keys = 512

    def body(turn, state):
        top, total, blend = state
        at = turn * step_keys
        k = lax.dynamic_slice_in_dim(key_rows, at, step_keys, 0)
        v = lax.dynamic_slice_in_dim(value_rows, at, step_keys, 0)
        s = jnp.einsum("tgd,sd->gts", grouped, k, preferred_element_type=jnp.float32) * DH**-0.5
        visible = positions[:, None] >= at + jnp.arange(step_keys, dtype=jnp.int32)[None, :]
        s = jnp.where(visible, s, NEG)
        newest = jnp.maximum(top, jnp.max(s, axis=-1))
        weights = jnp.where(visible, jnp.exp(s - newest[..., None]), 0.0)
        fading = jnp.exp(top - newest)
        total = total * fading + jnp.sum(weights, axis=-1)
        update = jnp.einsum("gts,sd->tgd", weights.astype(jnp.bfloat16), v,
                            preferred_element_type=jnp.float32)
        return newest, total, blend * jnp.transpose(fading)[..., None] + update

    initial = (jnp.full((per_head, count), NEG, jnp.float32),
               jnp.zeros((per_head, count), jnp.float32),
               jnp.zeros((count, per_head, DH), jnp.float32))
    turns = (first_row + count) // step_keys
    _, total, blend = lax.fori_loop(0, turns, body, initial)
    return (blend / jnp.transpose(total)[..., None]).astype(jnp.bfloat16).reshape(queries.shape)


def decode_rows(page_store, queries, new_keys, new_values, slot_table, lengths):
    group_size = HQ // KVH
    row_count = queries.shape[0]
    picked = page_store[slot_table].reshape(row_count, PPR * PAGE, 2, KVH, DH)
    cache_keys = picked[:, :, 0]
    cache_values = picked[:, :, 1]
    query_rows = queries.reshape(row_count, STEPS, KVH, group_size, DH)
    fresh_keys = new_keys.reshape(row_count, STEPS, KVH, DH)
    fresh_values = new_values.reshape(row_count, STEPS, KVH, DH)
    score_cache = jnp.einsum(
        "rtkgd,rskd->rkgts", query_rows, cache_keys, preferred_element_type=jnp.float32
    ) * DH ** (-0.5)
    score_fresh = jnp.einsum(
        "rtkgd,rukd->rkgtu", query_rows, fresh_keys, preferred_element_type=jnp.float32
    ) * DH ** (-0.5)
    live_cache = (jnp.arange(PPR * PAGE, dtype=jnp.int32)[None, :] < lengths[:, None])[
        :, None, None, None, :
    ]
    live_fresh = (
        jnp.arange(STEPS, dtype=jnp.int32)[:, None] >= jnp.arange(STEPS, dtype=jnp.int32)[None, :]
    )
    score_cache = jnp.where(live_cache, score_cache, NEG)
    score_fresh = jnp.where(live_fresh, score_fresh, NEG)
    row_max = jnp.maximum(jnp.max(score_cache, axis=-1), jnp.max(score_fresh, axis=-1))[..., None]
    weight_cache = jnp.where(live_cache, jnp.exp(score_cache - row_max), 0.0)
    weight_fresh = jnp.where(live_fresh, jnp.exp(score_fresh - row_max), 0.0)
    row_sum = jnp.sum(weight_cache, axis=-1) + jnp.sum(weight_fresh, axis=-1)
    blended = jnp.einsum(
        "rkgts,rskd->rtkgd", weight_cache.astype(jnp.bfloat16), cache_values,
        preferred_element_type=jnp.float32)
    blended = blended + jnp.einsum(
        "rkgtu,rukd->rtkgd", weight_fresh.astype(jnp.bfloat16), fresh_values,
        preferred_element_type=jnp.float32)
    blended = blended / jnp.transpose(row_sum, (0, 3, 1, 2))[..., None]
    return blended.astype(jnp.bfloat16).reshape(row_count, STEPS, HQ * DH)


def on_device(pre_q, pre_k, pre_v, routes, dec_q, dec_k, dec_v, table, ctx_len):
    blk = lax.axis_index("blk")
    pages = ROWS // PAGE
    owner = routes[:, 0]
    onehot = (owner[:, None] == jnp.arange(N_POOL, dtype=jnp.int32)[None, :]).astype(jnp.int32)
    rank = jnp.sum((jnp.cumsum(onehot, axis=0) - onehot) * onehot, axis=1)
    place = owner * CAP + rank
    selector = (place[None, :] == jnp.arange(N_POOL * CAP, dtype=jnp.int32)[:, None]).astype(
        jnp.bfloat16)
    both = jnp.concatenate([pre_k, pre_v], axis=1).reshape(pages, PAGE * DH)
    psend = jnp.dot(selector, both, preferred_element_type=jnp.float32).astype(jnp.bfloat16)
    psend = psend.reshape(N_POOL, CAP * PAGE, DH)
    kp = jnp.concatenate([pre_k[:HALF], pre_k[HALF:]], axis=1)
    tiles, pages_in, k_all, v_all, bound = fused(pre_q, kp, pre_v.T, psend)

    def fast(tiles, *unused):
        return tiles.reshape(4, 2, 2, 256, DH).transpose(0, 3, 1, 2, 4).reshape(ROWS, 4 * DH)

    def slow(tiles, k_all, v_all, pre_q):
        k = k_all.reshape(N_BLK, 2, HALF, 2, DH // 2).transpose(0, 3, 2, 1, 4)
        v = v_all.reshape(N_BLK, DH, ROWS).transpose(0, 2, 1)
        return online_attend(pre_q, blk * ROWS, k.reshape(N_BLK * ROWS, DH),
                             v.reshape(N_BLK * ROWS, DH))

    safe = jnp.max(bound) * SCALE2 <= SAFE
    prefill_out = lax.cond(safe, fast, slow, tiles, k_all, v_all, pre_q)

    store = pages_in.reshape(N_POOL, CAP, PAGE, 2, DH // 2)
    store = store.transpose(1, 2, 3, 0, 4).reshape(CAP, PAGE, 2, KVH * DH)
    decode_out = decode_rows(store, dec_q, dec_k, dec_v, table, ctx_len)
    return prefill_out, decode_out


def solution(mesh):
    in_specs = (
        P("blk", "pool"),
        P("blk", "pool"),
        P("blk", "pool"),
        P("blk", None),
        P(("blk", "pool"), None, None),
        P(("blk", "pool"), None, None),
        P(("blk", "pool"), None, None),
        P(("blk", "pool"), None),
        P(("blk", "pool")),
    )
    out_specs = (P("blk", "pool"), P(("blk", "pool"), None, None))
    return jax.shard_map(
        on_device, mesh=mesh, in_specs=in_specs, out_specs=out_specs, check_vma=False
    )
```

```python
import functools

import jax
import jax.numpy as jnp
from jax import lax
from jax.experimental import pallas as pl
from jax.experimental.pallas import tpu as pltpu
from jax.sharding import PartitionSpec as P

HQ = 32
KVH = 4
DH = 128
PAGE = 16
STEPS = 4
PPR = 8

N_BLK = 16
N_POOL = 8
Z = 4
ROWS = 1024
HALF = ROWS // 2
TILE = 512
TILES = 8
GUESTS = 4
SCALE2 = DH**-0.5 * 1.4426950408889634
SPLIT = 5
EARLY = 2
SAFE = 100.0
NEG = -1e30
MESH = pl.DeviceIdType.MESH

A1, A2, B1, B2, SIB, COPIES = 0, 2, 4, 12, 20, 36


def fused_kernel(q_ref, k_ref, v_ref, routes_ref, dq_ref, dk_ref, dv_ref, table_ref, ctx_ref,
                 out_ref, dec_ref, kall_ref, vall_ref, bound_ref,
                 qin, kbuf, vbuf, kun, zk, zv, qst, acc, ostage, kmx,
                 send, recv, qsend, qrecv, osend, orecv, zsend, zrecv, local):
    blk, pool = lax.axis_index("blk"), lax.axis_index("pool")
    core = lax.rem(blk, 2)
    cb = blk // 2
    x_hi, y = cb // 4, lax.rem(cb, 4)
    z, x_lo = pool // 2, lax.rem(pool, 2)
    mirror = N_BLK - 1 - blk

    def block_of(xh, yy):
        return (xh * 4 + yy) * 2 + core

    def along_x(k):
        return ((x_hi, x_lo), (x_hi, 1 - x_lo), (1 - x_hi, 1 - x_lo), (1 - x_hi, x_lo))[k]

    def along_y(k):
        return lax.rem(y + (0, 1, 3, 2)[k], 4)

    def device(kx, ky):
        xh, xl = along_x(kx)
        return (block_of(xh, along_y(ky)), z * 2 + xl)

    def at_z(d):
        return (blk, lax.rem(z + d, Z) * 2 + x_lo)

    sibling = (blk + 1 - 2 * core, pool)
    partner = (mirror, z * 2 + 1 - x_lo)

    barrier = pltpu.get_barrier_semaphore()
    peers = [device(1, 0), device(2, 0), device(0, 1), device(0, 2), sibling, partner]
    peers += [at_z(d) for d in range(1, Z)]
    for peer in peers:
        pl.semaphore_signal(barrier, inc=1, device_id=peer, device_id_type=MESH)
    q_in = pltpu.make_async_copy(q_ref, qin, local.at[0])
    q_in.start()

    kbuf[blk, x_lo] = jnp.concatenate([k_ref[:, :HALF], k_ref[:, HALF:]], axis=0).T
    vbuf[blk, x_lo] = v_ref[...]
    pl.semaphore_wait(barrier, len(peers))

    class Gather:
        def __init__(self, index, buf, rows, x_first):
            self.index, self.buf, self.rows, self.x_first = index, buf, rows, x_first

        def place(self, ka, kb):
            return (ka, kb) if self.x_first else (kb, ka)

        def piece(self, ka, kb, half=None):
            kx, ky = self.place(ka, kb)
            xh, xl = along_x(kx)
            whole = self.buf.at[block_of(xh, along_y(ky)), xl]
            if half is None:
                return whole
            return whole.at[pl.ds(half * self.rows // 2, self.rows // 2)]

        def copy(self, slot, ka, kb, half, to, there=None):
            there = slot if there is None else there
            ref = self.piece(ka, kb, half)
            return pltpu.make_async_remote_copy(
                src_ref=ref, dst_ref=ref,
                send_sem=send.at[self.index, slot], recv_sem=recv.at[self.index, there],
                device_id=to, device_id_type=MESH)

        def neighbour(self, axis, n):
            ka, kb = ((n + 1, 0), (0, n + 1))[axis]
            return device(*self.place(ka, kb))

        def seen(self, axis, n):
            is_x = (axis == 0) == self.x_first
            return n if is_x else 1 - n

        def all_copies(self):
            out = {}
            for n in range(2):
                out["a1", n] = lambda n=n: self.copy(
                    A1 + n, 0, 0, None, self.neighbour(0, n), A1 + self.seen(0, n))
                out["a2", n] = lambda n=n: self.copy(
                    A2 + n, 2 - n, 0, n, self.neighbour(0, n))
                for ka in range(4):
                    out["b1", ka, n] = lambda n=n, ka=ka: self.copy(
                        B1 + ka * 2 + n, ka, 0, None, self.neighbour(1, n),
                        B1 + ka * 2 + self.seen(1, n))
                    out["b2", ka, n] = lambda n=n, ka=ka: self.copy(
                        B2 + ka * 2 + n, ka, 2 - n, n, self.neighbour(1, n))
            for ka in range(4):
                for kb in range(4):
                    out["sib", ka, kb] = lambda ka=ka, kb=kb: self.copy(
                        SIB + ka * 4 + kb, ka, kb, None, sibling)
            return out

        def start(self, *key):
            self.all_copies()[key]().start()

        def arrive(self, slot, ka, kb, half=None):
            ref = self.piece(ka, kb, half)
            pltpu.make_async_remote_copy(
                src_ref=ref, dst_ref=ref, send_sem=send.at[self.index, slot],
                recv_sem=recv.at[self.index, slot], device_id=sibling,
                device_id_type=MESH).wait_recv()

        def got_a1(self, n):
            self.arrive(A1 + n, n + 1, 0)
            self.start("a2", 1 - n)
            self.start("sib", n + 1, 0)

        def pass_b1(self, ka):
            self.start("b1", ka, 0)
            self.start("b1", ka, 1)

        def got_a2(self):
            for half in range(2):
                self.arrive(A2 + half, 3, 0, half)
            self.start("sib", 3, 0)
            self.pass_b1(3)

        def got_b1(self, ka, n):
            self.arrive(B1 + ka * 2 + n, ka, n + 1)
            self.start("b2", ka, 1 - n)
            self.start("sib", ka, n + 1)

        def got_b2(self, ka):
            for half in range(2):
                self.arrive(B2 + ka * 2 + half, ka, 3, half)
            self.start("sib", ka, 3)

        def got_sib(self, ka, kb):
            kx, ky = self.place(ka, kb)
            xh, xl = along_x(kx)
            there = (xh * 4 + along_y(ky)) * 2 + 1 - core
            ref = self.buf.at[there, xl]
            slot = SIB + ka * 4 + kb
            pltpu.make_async_remote_copy(
                src_ref=ref, dst_ref=ref, send_sem=send.at[self.index, slot],
                recv_sem=recv.at[self.index, slot], device_id=sibling,
                device_id_type=MESH).wait_recv()

        def sib_xy(self, kx, ky):
            self.got_sib(*((kx, ky) if self.x_first else (ky, kx)))

        def finish(self):
            for make in self.all_copies().values():
                make().wait_send()

    keys = Gather(0, kbuf, HALF, True)
    values = Gather(1, vbuf, DH // 2, False)

    keys.start("a1", 0)
    values.start("b1", 0, 0)
    keys.start("sib", 0, 0)
    values.start("sib", 0, 0)
    keys.start("a1", 1)
    values.start("b1", 0, 1)
    for n in range(2):
        values.start("a1", n)
        keys.start("b1", 0, n)

    high = blk >= N_BLK // 2
    moved = (jnp.where(high, blk, mirror) - 7) // 2
    mine = jnp.where(high, TILES - moved, TILES)
    guests = jnp.where(high, 0, moved)
    sent_tiles = jnp.where(high, moved, 0)

    def q_copy(v):
        return pltpu.make_async_remote_copy(
            src_ref=qst.at[TILES - 1 - v], dst_ref=qst.at[TILES + v],
            send_sem=qsend.at[v], recv_sem=qrecv.at[v],
            device_id=partner, device_id_type=MESH)

    def out_part(u, h):
        row = pl.multiple_of(u // 2 * 256, 256)
        column = pl.multiple_of((lax.rem(u, 2) * 2 + h) * DH, DH)
        return out_ref.at[pl.ds(row, 256), pl.ds(column, DH)]

    def o_copy(v, h):
        return pltpu.make_async_remote_copy(
            src_ref=ostage.at[TILES + v, h], dst_ref=out_part(TILES - 1 - v, h),
            send_sem=osend.at[v, h], recv_sem=orecv.at[v, h],
            device_id=partner, device_id_type=MESH)

    def when_loop(count, body):
        def step(v, carry):
            body(v)
            return carry
        lax.fori_loop(0, count, step, 0)

    def z_copy(index, d):
        buf, there = ((kbuf, zk), (vbuf, zv))[index]
        return pltpu.make_async_remote_copy(
            src_ref=buf.at[blk], dst_ref=there.at[z],
            send_sem=zsend.at[index, d], recv_sem=zrecv.at[index, d],
            device_id=at_z(d), device_id_type=MESH)

    def z_arrive(index, d):
        ref = (zk, zv)[index].at[lax.rem(z + Z - d, Z)]
        pltpu.make_async_remote_copy(
            src_ref=ref, dst_ref=ref, send_sem=zsend.at[index, d], recv_sem=zrecv.at[index, d],
            device_id=sibling, device_id_type=MESH).wait_recv()

    def z_own(index):
        buf, there = ((kbuf, zk), (vbuf, zv))[index]
        return pltpu.make_async_copy(buf.at[blk], there.at[z], local.at[1 + index])

    d_in = lax.broadcasted_iota(jnp.int32, (DH, 4 * DH), 0)
    column = lax.broadcasted_iota(jnp.int32, (DH, 4 * DH), 1)
    half, lane = column // 256, lax.rem(column, 256)
    source = lax.rem(lane, 128) - 64 * half
    spread = jnp.where((source >= 0) & (source < 64) & (source + (lane // 128) * 64 == d_in),
                       1.0, 0.0).astype(jnp.bfloat16)

    def clear(u):
        acc[u] = jnp.zeros((144, TILE), jnp.float32)

    q_in.wait()
    for u in range(TILES):
        t, hp = u // 2, u % 2
        for h in range(2):
            col = (hp * 2 + h) * DH
            qst[u, h * 256:(h + 1) * 256, :] = qin[t * 256:(t + 1) * 256, col:col + DH]
    when_loop(sent_tiles, lambda v: q_copy(v).start())
    when_loop(TILES + GUESTS, clear)
    kmx[...] = jnp.zeros_like(kmx)

    ones = jnp.ones((16, HALF), jnp.bfloat16)

    def scores(u, block, h):
        return lax.dot_general(kun[block, h], qst[u], (((1,), (1,)), ((), ())),
                               preferred_element_type=jnp.float32)

    def mixed(s, block, h, visible=None):
        weights = jnp.exp2(s * SCALE2)
        if visible is not None:
            weights = jnp.where(visible, weights, 0.0)
        cut = slice(h * HALF, (h + 1) * HALF)
        values_in = jnp.concatenate([vbuf[block, 0, :, cut], vbuf[block, 1, :, cut], ones], axis=0)
        return jnp.dot(values_in, weights.astype(jnp.bfloat16), preferred_element_type=jnp.float32)

    def full(tiles, chunks):
        work = [(u, chunk) for u in tiles for chunk in chunks]
        ahead = scores(work[0][0], *work[0][1])
        total = None
        for i, (u, chunk) in enumerate(work):
            now = ahead
            if i + 1 < len(work):
                ahead = scores(work[i + 1][0], *work[i + 1][1])
            part = mixed(now, *chunk)
            total = part if i % len(chunks) == 0 else total + part
            if i % len(chunks) == len(chunks) - 1:
                acc[u] += total

    def chunks_of(at):
        return [(2 * at + core_at, h) for core_at in range(2) for h in range(2)]

    def diagonal(u, t, block):
        key_at = lax.broadcasted_iota(jnp.int32, (HALF, TILE), 0)
        row_at = lax.rem(lax.broadcasted_iota(jnp.int32, (HALF, TILE), 1), 256)
        late = t // 2
        visible = key_at <= row_at + (t - 2 * late) * 256

        @pl.when(late == 0)
        def _():
            acc[u] += mixed(scores(u, block, 0), block, 0, visible)

        @pl.when(late == 1)
        def _():
            first, second = scores(u, block, 0), scores(u, block, 1)
            acc[u] += mixed(first, block, 0) + mixed(second, block, 1, visible)

    def tile_turn(u, t, tile_block, at):
        tile_cb = tile_block // 2

        @pl.when(at < tile_cb)
        def _():
            full([u], chunks_of(at))

        @pl.when(at == tile_cb)
        def _():
            @pl.when(lax.rem(tile_block, 2) == 1)
            def _():
                full([u], [(2 * at, 0), (2 * at, 1)])
            diagonal(u, t, tile_block)

    def keep_copy(at, slot):
        ref, buf = ((kall_ref, kun), (vall_ref, vbuf))[slot]
        return pltpu.make_async_copy(buf.at[pl.ds(2 * at, 2)], ref.at[pl.ds(2 * at, 2)],
                                     local.at[3 + slot + 2 * at])

    def note_keys(at):
        for core_at in range(2):
            for xl in range(2):
                piece = jnp.concatenate(
                    [kbuf[2 * at + core_at, p, :, xl * 64:(xl + 1) * 64] for p in range(2)], axis=1)
                kun[2 * at + core_at, xl] = piece
                size = jnp.abs(piece.astype(jnp.float32)).reshape(HALF // 8, 8, DH)
                kmx[...] = jnp.maximum(kmx[...], jnp.max(size, axis=0))
        keep_copy(at, 0).start()
        keep_copy(at, 1).start()

    def take_guest(v):
        q_copy(v).wait_recv()

    def z_start():
        for index in range(2):
            z_own(index).start()
            for d in range(1, Z):
                z_copy(index, d).start()

    def both(method, *keys_of):
        for args in keys_of:
            for gather in (keys, values):
                getattr(gather, method)(*args)

    near, far = (0, 1), (2, 3)
    order = [(near, 0), (far, 0), (near, 1), (near, 2), (far, 1), (far, 2), (near, 3), (far, 3)]
    places = [along_x(pair[0])[0] * 4 + along_y(ky) for pair, ky in order]

    events = [
        (1, 0, 2, lambda: both("got_a2", ())),
        (1, 0, 99, lambda: both("got_b2", (0,))),
        (2, 1, 1, lambda: both("got_b1", (1, 0), (1, 1))),
        (3, 1, 2, lambda: both("got_b1", (2, 0), (2, 1))),
        (4, 1, 3, z_start),
        (4, 1, 5, lambda: both("got_b1", (3, 0), (3, 1))),
        (4, 1, 6, lambda: both("got_b2", (1,), (2,))),
        (SPLIT, 1, 8, lambda: both("got_b2", (3,))),
    ]

    keys.got_a1(0)
    keys.pass_b1(1)
    values.got_a1(0)
    values.pass_b1(1)
    values.got_a1(1)
    keys.got_a1(1)
    values.got_b1(0, 0)
    keys.got_b1(0, 0)
    keys.got_b1(0, 1)
    values.got_b1(0, 1)
    keys.pass_b1(2)
    values.pass_b1(2)

    def result(u):
        total = acc[u]
        ostage[u] = (total[:DH] / total[DH:DH + 1]).T.astype(jnp.bfloat16).reshape(2, 256, DH)

    def own_out(u, h):
        return pltpu.make_async_copy(ostage.at[u, h], out_part(u, h), local.at[19 + 2 * u + h])

    def place_at(tau):
        at = places[0]
        for k in range(1, len(places)):
            at = jnp.where(tau == k, places[k], at)
        return at

    def arrived(pair, ky):
        for kx in pair:
            keys.sib_xy(kx, ky)
            values.sib_xy(kx, ky)

    def turn(tau, done):
        finishing = tau >= SPLIT
        for turn_of, since, number, event in events:
            pl.when((tau == turn_of) & (done[since] <= number))(event)
        for k, (pair, ky) in enumerate(order):
            @pl.when(tau == min(k, SPLIT))
            def _(pair=pair, ky=ky):
                arrived(pair, ky)

        @pl.when(tau < SPLIT)
        def _():
            note_keys(place_at(tau))

        @pl.when(tau == SPLIT)
        def _():
            lax.fori_loop(SPLIT, len(order), lambda k, c: (note_keys(place_at(k)), c)[1], 0)

        at_now = place_at(tau)
        own_count = jnp.where(at_now <= cb, mine, 0)
        here = jnp.where(tau == 0, jnp.minimum(guests, EARLY), guests)
        count = own_count + jnp.where(at_now <= mirror // 2, here, 0)
        first = 2 * (tau - SPLIT)
        remain = len(order) - SPLIT
        late_guests = (first >= EARLY) & (first < guests)
        steps = jnp.where(finishing, remain + jnp.where(late_guests, 1, 0), (count + 1) // 2)

        def tile_at(index):
            guest = jnp.where(finishing, index < guests, index >= own_count)
            v = jnp.where(finishing, index, index - own_count)
            own = jnp.where(finishing, index - guests, index)
            return (guest, v, jnp.where(guest, TILES + v, own),
                    jnp.where(guest, TILES - 1 - v, own) // 2, jnp.where(guest, mirror, blk))

        def item(i, carry):
            for turn_of, since, number, event in events:
                pl.when((tau >= since) & (tau < turn_of) & (done[since] + i == number))(event)
            at = place_at(jnp.where(finishing, lax.rem(SPLIT + i, len(order)), tau))
            index = jnp.where(finishing, first, 2 * i)
            limit = jnp.where(finishing, jnp.where(i < remain, guests + mine, guests), count)
            lone = index + 1 >= limit
            guest_0, v_0, u_0, _, block_0 = tile_at(index)
            guest_1, v_1, u_1, _, block_1 = tile_at(index + 1)
            for guest, v, here in ((guest_0, v_0, True), (guest_1, v_1, jnp.logical_not(lone))):
                @pl.when(here & guest & (tau == jnp.where(v >= EARLY, 1, 0)))
                def _(v=v):
                    take_guest(v)
            pair = jnp.logical_not(lone) & (at < block_0 // 2) & (at < block_1 // 2)

            @pl.when(pair)
            def _():
                full([u_0, u_1], chunks_of(at))

            @pl.when(jnp.logical_not(pair))
            def _():
                def single(k, c):
                    _, _, u, t, block = tile_at(index + k)
                    tile_turn(u, t, block, at)
                    return c
                lax.fori_loop(0, jnp.where(lone, 1, 2), single, 0)
            return carry

        lax.fori_loop(0, steps, item, 0)

        @pl.when(finishing)
        def _():
            def end(k, c):
                guest, v, u, _, _ = tile_at(first + k)
                result(u)
                for h in range(2):
                    pl.when(guest)(lambda h=h: o_copy(v, h).start())
                    pl.when(jnp.logical_not(guest))(lambda h=h: own_out(u, h).start())
                return c
            lax.fori_loop(0, jnp.minimum(guests + mine - first, 2), end, 0)
        return (done[0] + jnp.where(finishing, 0, steps),
                done[1] + jnp.where(finishing | (tau == 0), 0, steps))

    lax.fori_loop(0, SPLIT + (guests + mine + 1) // 2, turn, (0, 0))

    kk = jnp.broadcast_to(jnp.max(kmx[...], axis=0, keepdims=True), (16, DH)).astype(jnp.bfloat16)

    def reach(u, farthest):
        far_score = lax.dot_general(kk, jnp.abs(qst[u]), (((1,), (1,)), ((), ())),
                                    preferred_element_type=jnp.float32)
        return jnp.maximum(farthest, far_score)

    farthest = lax.fori_loop(0, TILES, reach, jnp.zeros((16, TILE), jnp.float32))
    bound_ref[0, 0] = jnp.max(farthest)

    for index in range(2):
        z_own(index).wait()
        for d in range(1, Z):
            z_arrive(index, d)
    owned = (jnp.broadcast_to(routes_ref[...], (16, 64)) == pool).astype(jnp.float32)
    page_at = lax.broadcasted_iota(jnp.int32, (64, ROWS), 0)
    token_page = lax.broadcasted_iota(jnp.int32, (64, ROWS), 1) // PAGE
    pick = owned.astype(jnp.bfloat16)
    rank = jnp.dot(pick, (page_at < token_page).astype(jnp.float32).astype(jnp.bfloat16),
                   preferred_element_type=jnp.float32)
    held = jnp.dot(pick, (page_at == token_page).astype(jnp.float32).astype(jnp.bfloat16),
                   preferred_element_type=jnp.float32)
    slot = jnp.where(held > 0, rank, -1.0)
    filled = jnp.sum(owned, axis=1, keepdims=True)
    row_of = lax.broadcasted_iota(jnp.int32, (16, ROWS), 0) // STEPS
    in_page = lax.rem(lax.broadcasted_iota(jnp.int32, (16, ROWS), 1), PAGE)

    def by_row(values_of):
        out = jnp.full((16, ROWS), values_of[0], jnp.int32)
        for r in range(1, 4):
            out = jnp.where(row_of == r, values_of[r], out)
        return out

    allowed = by_row([ctx_ref[r] for r in range(4)])
    times = jnp.zeros((16, ROWS), jnp.float32)
    blank = jnp.zeros((16, 1), jnp.float32)
    for p in range(PPR):
        named = by_row([table_ref[r, p] for r in range(4)]).astype(jnp.float32)
        times += jnp.where((named == slot) & (p * PAGE + in_page < allowed), 1.0, 0.0)
        shown = jnp.clip(allowed[:, :1] - p * PAGE, 0, PAGE).astype(jnp.float32)
        blank += jnp.where(named[:, :1] >= filled, shown, 0.0)
    often = [jnp.concatenate([times[:, h * HALF:(h + 1) * HALF]] * 8, axis=0) for h in range(2)]
    blank = jnp.concatenate([blank] * 8, axis=0)
    new_row = lax.broadcasted_iota(jnp.int32, (8 * 16, 16), 0)
    new_col = lax.broadcasted_iota(jnp.int32, (8 * 16, 16), 1)
    fresh = ((lax.rem(new_row, 16) // STEPS == new_col // STEPS)
             & (lax.rem(new_col, STEPS) <= lax.rem(new_row, STEPS)))
    nt = (((1,), (1,)), ((), ()))

    def dot_nt(a, b):
        return lax.dot_general(a, b, nt, preferred_element_type=jnp.float32)

    def rows_of(ref):
        return jnp.concatenate([ref[r].astype(jnp.float32) for r in range(4)], axis=0).astype(
            jnp.bfloat16)

    dq_all, dk_all, dv_all = rows_of(dq_ref), rows_of(dk_ref), rows_of(dv_ref)
    for g in range(KVH):
        queries = jnp.concatenate(
            [dq_all[:, (g * 8 + h) * DH:(g * 8 + h + 1) * DH] for h in range(8)], axis=0)
        wide = jnp.dot(queries, spread, preferred_element_type=jnp.float32).astype(jnp.bfloat16)
        keys_in = jnp.concatenate([zk[g, 0], zk[g, 1]], axis=1)
        values_in = jnp.concatenate([zv[g, 0], zv[g, 1]], axis=0)
        cut = slice(g * DH, (g + 1) * DH)
        s = [dot_nt(wide[:, h * 256:(h + 1) * 256], keys_in) * SCALE2 for h in range(2)]
        s_new = dot_nt(queries, dk_all[:, cut]) * SCALE2
        top = jnp.maximum(jnp.max(jnp.where(fresh, s_new, NEG), axis=1, keepdims=True),
                          jnp.where(blank > 0, 0.0, NEG))
        for h in range(2):
            top = jnp.maximum(top, jnp.max(jnp.where(often[h] > 0, s[h], NEG), axis=1, keepdims=True))
        w_new = jnp.where(fresh, jnp.exp2(s_new - top), 0.0)
        total = jnp.sum(w_new, axis=1, keepdims=True)
        total += jnp.where(blank > 0, blank * jnp.exp2(jnp.minimum(-top, 0.0)), 0.0)
        blend = jnp.dot(w_new.astype(jnp.bfloat16), dv_all[:, cut], preferred_element_type=jnp.float32)
        for h in range(2):
            w = jnp.where(often[h] > 0, jnp.exp2(s[h] - top), 0.0) * often[h]
            total += jnp.sum(w, axis=1, keepdims=True)
            blend += dot_nt(w.astype(jnp.bfloat16), values_in[:, h * HALF:(h + 1) * HALF])
        done = blend / total
        for h in range(8):
            for r in range(4):
                dec_ref[r, :, (g * 8 + h) * DH:(g * 8 + h + 1) * DH] = done[
                    h * 16 + r * 4:h * 16 + r * 4 + 4].astype(jnp.bfloat16)

    for index in range(2):
        for d in range(1, Z):
            z_copy(index, d).wait_send()
    when_loop(sent_tiles, lambda v: q_copy(v).wait_send())
    keys.finish()
    values.finish()
    for at in range(N_BLK // 2):
        keep_copy(at, 0).wait()
        keep_copy(at, 1).wait()
    for h in range(2):
        when_loop(mine, lambda u, h=h: own_out(u, h).wait())
        when_loop(guests, lambda v, h=h: o_copy(v, h).wait_send())
        when_loop(sent_tiles, lambda v, h=h: o_copy(v, h).wait_recv())


def fused(*args):
    vmem = pl.BlockSpec(memory_space=pltpu.VMEM)
    smem = pl.BlockSpec(memory_space=pltpu.SMEM)
    anywhere = pl.BlockSpec(memory_space=pl.ANY)
    bf16, f32 = jnp.bfloat16, jnp.float32
    slots = TILES + GUESTS
    return pl.pallas_call(
        fused_kernel,
        out_shape=(
            jax.ShapeDtypeStruct((ROWS, 4 * DH), bf16),
            jax.ShapeDtypeStruct((4, STEPS, HQ * DH), bf16),
            jax.ShapeDtypeStruct((N_BLK, 2, HALF, DH), bf16),
            jax.ShapeDtypeStruct((N_BLK, 2, DH // 2, ROWS), bf16),
            jax.ShapeDtypeStruct((1, 1), f32),
        ),
        in_specs=[anywhere] + [vmem] * 6 + [smem] * 2,
        out_specs=(anywhere, vmem, anywhere, anywhere, smem),
        scratch_shapes=[
            pltpu.VMEM((ROWS, 4 * DH), bf16),
            pltpu.VMEM((N_BLK, 2, HALF, DH), bf16),
            pltpu.VMEM((N_BLK, 2, DH // 2, ROWS), bf16),
            pltpu.VMEM((N_BLK, 2, HALF, DH), bf16),
            pltpu.VMEM((Z, 2, HALF, DH), bf16),
            pltpu.VMEM((Z, 2, DH // 2, ROWS), bf16),
            pltpu.VMEM((slots, TILE, DH), bf16),
            pltpu.VMEM((slots, 144, TILE), f32),
            pltpu.VMEM((slots, 2, 256, DH), bf16),
            pltpu.VMEM((8, DH), f32),
            pltpu.SemaphoreType.DMA((2, COPIES)),
            pltpu.SemaphoreType.DMA((2, COPIES)),
            pltpu.SemaphoreType.DMA((GUESTS,)),
            pltpu.SemaphoreType.DMA((GUESTS,)),
            pltpu.SemaphoreType.DMA((GUESTS, 2)),
            pltpu.SemaphoreType.DMA((GUESTS, 2)),
            pltpu.SemaphoreType.DMA((2, Z)),
            pltpu.SemaphoreType.DMA((2, Z)),
            pltpu.SemaphoreType.DMA((19 + 2 * TILES,)),
        ],
        compiler_params=pltpu.CompilerParams(
            collective_id=0, has_side_effects=True, vmem_limit_bytes=56 << 20),
        cost_estimate=pl.CostEstimate(flops=2 * 10**10, bytes_accessed=2 * 10**7,
                                      transcendentals=4 * 10**7),
        name="prefill",
    )(*args)


def online_attend(queries, first_row, key_rows, value_rows):
    count, length = queries.shape[0], key_rows.shape[0]
    per_head = queries.shape[1] // DH
    grouped = queries.reshape(count, per_head, DH)
    positions = first_row + jnp.arange(count, dtype=jnp.int32)
    step_keys = 512

    def body(turn, state):
        top, total, blend = state
        at = turn * step_keys
        k = lax.dynamic_slice_in_dim(key_rows, at, step_keys, 0)
        v = lax.dynamic_slice_in_dim(value_rows, at, step_keys, 0)
        s = jnp.einsum("tgd,sd->gts", grouped, k, preferred_element_type=jnp.float32) * DH**-0.5
        visible = positions[:, None] >= at + jnp.arange(step_keys, dtype=jnp.int32)[None, :]
        s = jnp.where(visible, s, NEG)
        newest = jnp.maximum(top, jnp.max(s, axis=-1))
        weights = jnp.where(visible, jnp.exp(s - newest[..., None]), 0.0)
        fading = jnp.exp(top - newest)
        total = total * fading + jnp.sum(weights, axis=-1)
        update = jnp.einsum("gts,sd->tgd", weights.astype(jnp.bfloat16), v,
                            preferred_element_type=jnp.float32)
        return newest, total, blend * jnp.transpose(fading)[..., None] + update

    initial = (jnp.full((per_head, count), NEG, jnp.float32),
               jnp.zeros((per_head, count), jnp.float32),
               jnp.zeros((count, per_head, DH), jnp.float32))
    turns = (first_row + count) // step_keys
    _, total, blend = lax.fori_loop(0, turns, body, initial)
    return (blend / jnp.transpose(total)[..., None]).astype(jnp.bfloat16).reshape(queries.shape)


def on_device(pre_q, pre_k, pre_v, routes, dec_q, dec_k, dec_v, table, ctx_len):
    blk = lax.axis_index("blk")
    prefill_out, decode_out, k_all, v_all, bound = fused(
        pre_q, pre_k.T, pre_v.T, routes.T, dec_q, dec_k, dec_v, table, ctx_len)

    def slow(prefill_out, k_all, v_all, pre_q):
        v = v_all.reshape(N_BLK, DH, ROWS).transpose(0, 2, 1)
        return online_attend(pre_q, blk * ROWS, k_all.reshape(N_BLK * ROWS, DH),
                             v.reshape(N_BLK * ROWS, DH))

    safe = bound[0, 0] * SCALE2 <= SAFE
    prefill_out = lax.cond(safe, lambda done, *unused: done, slow,
                           prefill_out, k_all, v_all, pre_q)
    return prefill_out, decode_out


def solution(mesh):
    in_specs = (
        P("blk", "pool"),
        P("blk", "pool"),
        P("blk", "pool"),
        P("blk", None),
        P(("blk", "pool"), None, None),
        P(("blk", "pool"), None, None),
        P(("blk", "pool"), None, None),
        P(("blk", "pool"), None),
        P(("blk", "pool")),
    )
    out_specs = (P("blk", "pool"), P(("blk", "pool"), None, None))
    return jax.shard_map(
        on_device, mesh=mesh, in_specs=in_specs, out_specs=out_specs, check_vma=False
    )
```

```python
import functools

import jax
import jax.numpy as jnp
from jax import lax
from jax.experimental import pallas as pl
from jax.experimental.pallas import tpu as pltpu
from jax.sharding import PartitionSpec as P

HQ = 32
KVH = 4
DH = 128
PAGE = 16
STEPS = 4
PPR = 8

N_BLK = 16
N_POOL = 8
Z = 4
ROWS = 1024
HALF = ROWS // 2
TILE = 512
TILES = 8
GUESTS = 4
SCALE2 = DH**-0.5 * 1.4426950408889634
SPLIT = 7
EARLY = 2
SAFE = 100.0
NEG = -1e30
MESH = pl.DeviceIdType.MESH

A1, A2, B1, B2, SIB, COPIES = 0, 2, 4, 12, 20, 36


def fused_kernel(q_ref, k_ref, v_ref, routes_ref, dq_ref, dk_ref, dv_ref, table_ref, ctx_ref,
                 out_ref, dec_ref, kall_ref, vall_ref, bound_ref,
                 qin, kbuf, vbuf, kun, zk, zv, qst, acc, ostage, kmx,
                 send, recv, qsend, qrecv, osend, orecv, zsend, zrecv, local):
    blk, pool = lax.axis_index("blk"), lax.axis_index("pool")
    core = lax.rem(blk, 2)
    cb = blk // 2
    x_hi, y = cb // 4, lax.rem(cb, 4)
    z, x_lo = pool // 2, lax.rem(pool, 2)
    mirror = N_BLK - 1 - blk

    def block_of(xh, yy):
        return (xh * 4 + yy) * 2 + core

    def along_x(k):
        return ((x_hi, x_lo), (x_hi, 1 - x_lo), (1 - x_hi, 1 - x_lo), (1 - x_hi, x_lo))[k]

    def along_y(k):
        return lax.rem(y + (0, 1, 3, 2)[k], 4)

    def device(kx, ky):
        xh, xl = along_x(kx)
        return (block_of(xh, along_y(ky)), z * 2 + xl)

    def at_z(d):
        return (blk, lax.rem(z + d, Z) * 2 + x_lo)

    sibling = (blk + 1 - 2 * core, pool)
    partner = (mirror, z * 2 + 1 - x_lo)

    barrier = pltpu.get_barrier_semaphore()
    peers = [device(1, 0), device(2, 0), device(0, 1), device(0, 2), sibling, partner]
    peers += [at_z(d) for d in range(1, Z)]
    for peer in peers:
        pl.semaphore_signal(barrier, inc=1, device_id=peer, device_id_type=MESH)
    q_in = pltpu.make_async_copy(q_ref, qin, local.at[0])
    q_in.start()

    kbuf[blk, x_lo] = jnp.concatenate([k_ref[:, :HALF], k_ref[:, HALF:]], axis=0).T
    vbuf[blk, x_lo] = v_ref[...]
    pl.semaphore_wait(barrier, len(peers))

    class Gather:
        def __init__(self, index, buf, rows, x_first):
            self.index, self.buf, self.rows, self.x_first = index, buf, rows, x_first

        def place(self, ka, kb):
            return (ka, kb) if self.x_first else (kb, ka)

        def piece(self, ka, kb, half=None):
            kx, ky = self.place(ka, kb)
            xh, xl = along_x(kx)
            whole = self.buf.at[block_of(xh, along_y(ky)), xl]
            if half is None:
                return whole
            return whole.at[pl.ds(half * self.rows // 2, self.rows // 2)]

        def copy(self, slot, ka, kb, half, to, there=None):
            there = slot if there is None else there
            ref = self.piece(ka, kb, half)
            return pltpu.make_async_remote_copy(
                src_ref=ref, dst_ref=ref,
                send_sem=send.at[self.index, slot], recv_sem=recv.at[self.index, there],
                device_id=to, device_id_type=MESH)

        def neighbour(self, axis, n):
            ka, kb = ((n + 1, 0), (0, n + 1))[axis]
            return device(*self.place(ka, kb))

        def seen(self, axis, n):
            is_x = (axis == 0) == self.x_first
            return n if is_x else 1 - n

        def all_copies(self):
            out = {}
            for n in range(2):
                out["a1", n] = lambda n=n: self.copy(
                    A1 + n, 0, 0, None, self.neighbour(0, n), A1 + self.seen(0, n))
                out["a2", n] = lambda n=n: self.copy(
                    A2 + n, 2 - n, 0, n, self.neighbour(0, n))
                for ka in range(4):
                    out["b1", ka, n] = lambda n=n, ka=ka: self.copy(
                        B1 + ka * 2 + n, ka, 0, None, self.neighbour(1, n),
                        B1 + ka * 2 + self.seen(1, n))
                    out["b2", ka, n] = lambda n=n, ka=ka: self.copy(
                        B2 + ka * 2 + n, ka, 2 - n, n, self.neighbour(1, n))
            for ka in range(4):
                for kb in range(4):
                    out["sib", ka, kb] = lambda ka=ka, kb=kb: self.copy(
                        SIB + ka * 4 + kb, ka, kb, None, sibling)
            return out

        def start(self, *key):
            self.all_copies()[key]().start()

        def arrive(self, slot, ka, kb, half=None):
            ref = self.piece(ka, kb, half)
            pltpu.make_async_remote_copy(
                src_ref=ref, dst_ref=ref, send_sem=send.at[self.index, slot],
                recv_sem=recv.at[self.index, slot], device_id=sibling,
                device_id_type=MESH).wait_recv()

        def got_a1(self, n):
            self.arrive(A1 + n, n + 1, 0)
            self.start("a2", 1 - n)
            self.start("sib", n + 1, 0)

        def pass_b1(self, ka):
            self.start("b1", ka, 0)
            self.start("b1", ka, 1)

        def got_a2(self):
            for half in range(2):
                self.arrive(A2 + half, 3, 0, half)
            self.start("sib", 3, 0)
            self.pass_b1(3)

        def got_b1(self, ka, n):
            self.arrive(B1 + ka * 2 + n, ka, n + 1)
            self.start("b2", ka, 1 - n)
            self.start("sib", ka, n + 1)

        def got_b2(self, ka):
            for half in range(2):
                self.arrive(B2 + ka * 2 + half, ka, 3, half)
            self.start("sib", ka, 3)

        def got_sib(self, ka, kb):
            kx, ky = self.place(ka, kb)
            xh, xl = along_x(kx)
            there = (xh * 4 + along_y(ky)) * 2 + 1 - core
            ref = self.buf.at[there, xl]
            slot = SIB + ka * 4 + kb
            pltpu.make_async_remote_copy(
                src_ref=ref, dst_ref=ref, send_sem=send.at[self.index, slot],
                recv_sem=recv.at[self.index, slot], device_id=sibling,
                device_id_type=MESH).wait_recv()

        def sib_xy(self, kx, ky):
            self.got_sib(*((kx, ky) if self.x_first else (ky, kx)))

        def finish(self):
            for make in self.all_copies().values():
                make().wait_send()

    keys = Gather(0, kbuf, HALF, True)
    values = Gather(1, vbuf, DH // 2, False)

    keys.start("a1", 0)
    values.start("b1", 0, 0)
    keys.start("sib", 0, 0)
    values.start("sib", 0, 0)
    keys.start("a1", 1)
    values.start("b1", 0, 1)
    for n in range(2):
        values.start("a1", n)
        keys.start("b1", 0, n)

    high = blk >= N_BLK // 2
    moved = (jnp.where(high, blk, mirror) - 8) // 2
    mine = jnp.where(high, TILES - moved, TILES)
    guests = jnp.where(high, 0, moved)
    sent_tiles = jnp.where(high, moved, 0)

    def q_copy(v):
        return pltpu.make_async_remote_copy(
            src_ref=qst.at[TILES - 1 - v], dst_ref=qst.at[TILES + v],
            send_sem=qsend.at[v], recv_sem=qrecv.at[v],
            device_id=partner, device_id_type=MESH)

    def out_part(u, h):
        row = pl.multiple_of(u // 2 * 256, 256)
        column = pl.multiple_of((lax.rem(u, 2) * 2 + h) * DH, DH)
        return out_ref.at[pl.ds(row, 256), pl.ds(column, DH)]

    def o_copy(v, h):
        return pltpu.make_async_remote_copy(
            src_ref=ostage.at[TILES + v, h], dst_ref=out_part(TILES - 1 - v, h),
            send_sem=osend.at[v, h], recv_sem=orecv.at[v, h],
            device_id=partner, device_id_type=MESH)

    def when_loop(count, body):
        def step(v, carry):
            body(v)
            return carry
        lax.fori_loop(0, count, step, 0)

    def z_copy(index, d):
        buf, there = ((kbuf, zk), (vbuf, zv))[index]
        return pltpu.make_async_remote_copy(
            src_ref=buf.at[blk], dst_ref=there.at[z],
            send_sem=zsend.at[index, d], recv_sem=zrecv.at[index, d],
            device_id=at_z(d), device_id_type=MESH)

    def z_arrive(index, d):
        ref = (zk, zv)[index].at[lax.rem(z + Z - d, Z)]
        pltpu.make_async_remote_copy(
            src_ref=ref, dst_ref=ref, send_sem=zsend.at[index, d], recv_sem=zrecv.at[index, d],
            device_id=sibling, device_id_type=MESH).wait_recv()

    def z_own(index):
        buf, there = ((kbuf, zk), (vbuf, zv))[index]
        return pltpu.make_async_copy(buf.at[blk], there.at[z], local.at[1 + index])

    d_in = lax.broadcasted_iota(jnp.int32, (DH, 4 * DH), 0)
    column = lax.broadcasted_iota(jnp.int32, (DH, 4 * DH), 1)
    half, lane = column // 256, lax.rem(column, 256)
    source = lax.rem(lane, 128) - 64 * half
    spread = jnp.where((source >= 0) & (source < 64) & (source + (lane // 128) * 64 == d_in),
                       1.0, 0.0).astype(jnp.bfloat16)

    def clear(u):
        acc[u] = jnp.zeros((144, TILE), jnp.float32)

    q_in.wait()
    for u in range(TILES):
        t, hp = u // 2, u % 2
        for h in range(2):
            col = (hp * 2 + h) * DH
            qst[u, h * 256:(h + 1) * 256, :] = qin[t * 256:(t + 1) * 256, col:col + DH]
    when_loop(TILES + GUESTS, clear)
    kmx[...] = jnp.zeros_like(kmx)

    ones = jnp.ones((16, HALF), jnp.bfloat16)

    def scores(u, block, h):
        return lax.dot_general(kun[block, h], qst[u], (((1,), (1,)), ((), ())),
                               preferred_element_type=jnp.float32)

    def mixed(s, block, h, visible=None):
        weights = jnp.exp2(s * SCALE2)
        if visible is not None:
            weights = jnp.where(visible, weights, 0.0)
        cut = slice(h * HALF, (h + 1) * HALF)
        values_in = jnp.concatenate([vbuf[block, 0, :, cut], vbuf[block, 1, :, cut], ones], axis=0)
        return jnp.dot(values_in, weights.astype(jnp.bfloat16), preferred_element_type=jnp.float32)

    def full(tiles, chunks):
        work = [(u, chunk) for u in tiles for chunk in chunks]
        ahead = scores(work[0][0], *work[0][1])
        total = None
        for i, (u, chunk) in enumerate(work):
            now = ahead
            if i + 1 < len(work):
                ahead = scores(work[i + 1][0], *work[i + 1][1])
            part = mixed(now, *chunk)
            total = part if i % len(chunks) == 0 else total + part
            if i % len(chunks) == len(chunks) - 1:
                acc[u] += total

    def chunks_of(at):
        return [(2 * at + core_at, h) for core_at in range(2) for h in range(2)]

    def diagonal(tiles, t, block):
        key_at = lax.broadcasted_iota(jnp.int32, (HALF, TILE), 0)
        row_at = lax.rem(lax.broadcasted_iota(jnp.int32, (HALF, TILE), 1), 256)
        late = t // 2
        visible = key_at <= row_at + (t - 2 * late) * 256

        @pl.when(late == 0)
        def _():
            ahead = [scores(u, block, 0) for u in tiles]
            for u, s in zip(tiles, ahead):
                acc[u] += mixed(s, block, 0, visible)

        @pl.when(late == 1)
        def _():
            ahead = [scores(u, block, h) for u in tiles for h in range(2)]
            for i, u in enumerate(tiles):
                acc[u] += (mixed(ahead[2 * i], block, 0)
                           + mixed(ahead[2 * i + 1], block, 1, visible))

    def tile_turn(tiles, t, tile_block, at):
        tile_cb = tile_block // 2

        @pl.when(at < tile_cb)
        def _():
            full(tiles, chunks_of(at))

        @pl.when(at == tile_cb)
        def _():
            @pl.when(lax.rem(tile_block, 2) == 1)
            def _():
                full(tiles, [(2 * at, 0), (2 * at, 1)])
            diagonal(tiles, t, tile_block)

    def keep_copy(at, slot):
        ref, buf = ((kall_ref, kun), (vall_ref, vbuf))[slot]
        return pltpu.make_async_copy(buf.at[pl.ds(2 * at, 2)], ref.at[pl.ds(2 * at, 2)],
                                     local.at[3 + slot + 2 * at])

    def note_keys(at):
        for core_at in range(2):
            for xl in range(2):
                piece = jnp.concatenate(
                    [kbuf[2 * at + core_at, p, :, xl * 64:(xl + 1) * 64] for p in range(2)], axis=1)
                kun[2 * at + core_at, xl] = piece
                size = jnp.abs(piece.astype(jnp.float32)).reshape(HALF // 8, 8, DH)
                kmx[...] = jnp.maximum(kmx[...], jnp.max(size, axis=0))
        keep_copy(at, 0).start()
        keep_copy(at, 1).start()

    def take_guest(v):
        q_copy(v).wait_recv()

    def z_start():
        for index in range(2):
            z_own(index).start()
            for d in range(1, Z):
                z_copy(index, d).start()

    def both(method, *keys_of):
        for args in keys_of:
            for gather in (keys, values):
                getattr(gather, method)(*args)

    near, far = (0, 1), (2, 3)
    order = [(near, 0), (far, 0), (near, 1), (near, 2), (far, 1), (far, 2), (near, 3), (far, 3)]
    places = [along_x(pair[0])[0] * 4 + along_y(ky) for pair, ky in order]

    events = [
        (1, 0, 1, z_start),
        (1, 0, 1, lambda: both("got_a2", ())),
        (1, 0, 4, lambda: both("got_b1", (1, 0), (1, 1))),
        (1, 0, 99, lambda: both("got_b2", (0,))),
        (3, 1, 1, lambda: both("got_b1", (2, 0), (2, 1))),
        (4, 1, 4, lambda: both("got_b1", (3, 0), (3, 1))),
        (4, 1, 5, lambda: both("got_b2", (1,), (2,))),
        (SPLIT, 1, 8, lambda: both("got_b2", (3,))),
    ]

    keys.got_a1(0)
    keys.pass_b1(1)
    values.got_a1(0)
    values.pass_b1(1)
    values.got_a1(1)
    keys.got_a1(1)
    values.got_b1(0, 0)
    keys.got_b1(0, 0)
    keys.got_b1(0, 1)
    values.got_b1(0, 1)
    keys.pass_b1(2)
    values.pass_b1(2)

    when_loop(sent_tiles, lambda v: q_copy(v).start())

    def result(u):
        total = acc[u]
        ostage[u] = (total[:DH] / total[DH:DH + 1]).T.astype(jnp.bfloat16).reshape(2, 256, DH)

    def own_out(u, h):
        return pltpu.make_async_copy(ostage.at[u, h], out_part(u, h), local.at[19 + 2 * u + h])

    def place_at(tau):
        at = places[0]
        for k in range(1, len(places)):
            at = jnp.where(tau == k, places[k], at)
        return at

    def arrived(pair, ky):
        for kx in pair:
            keys.sib_xy(kx, ky)
            values.sib_xy(kx, ky)

    def decode():
        for index in range(2):
            z_own(index).wait()
            for d in range(1, Z):
                z_arrive(index, d)
        owned = (jnp.broadcast_to(routes_ref[...], (16, 64)) == pool).astype(jnp.float32)
        page_at = lax.broadcasted_iota(jnp.int32, (64, ROWS), 0)
        token_page = lax.broadcasted_iota(jnp.int32, (64, ROWS), 1) // PAGE
        pick = owned.astype(jnp.bfloat16)
        rank = jnp.dot(pick, (page_at < token_page).astype(jnp.float32).astype(jnp.bfloat16),
                       preferred_element_type=jnp.float32)
        held = jnp.dot(pick, (page_at == token_page).astype(jnp.float32).astype(jnp.bfloat16),
                       preferred_element_type=jnp.float32)
        slot = jnp.where(held > 0, rank, -1.0)
        filled = jnp.sum(owned, axis=1, keepdims=True)
        row_of = lax.broadcasted_iota(jnp.int32, (16, ROWS), 0) // STEPS
        in_page = lax.rem(lax.broadcasted_iota(jnp.int32, (16, ROWS), 1), PAGE)

        def by_row(values_of):
            out = jnp.full((16, ROWS), values_of[0], jnp.int32)
            for r in range(1, 4):
                out = jnp.where(row_of == r, values_of[r], out)
            return out

        allowed = by_row([ctx_ref[r] for r in range(4)])
        times = jnp.zeros((16, ROWS), jnp.float32)
        blank = jnp.zeros((16, 1), jnp.float32)
        for p in range(PPR):
            named = by_row([table_ref[r, p] for r in range(4)]).astype(jnp.float32)
            times += jnp.where((named == slot) & (p * PAGE + in_page < allowed), 1.0, 0.0)
            shown = jnp.clip(allowed[:, :1] - p * PAGE, 0, PAGE).astype(jnp.float32)
            blank += jnp.where(named[:, :1] >= filled, shown, 0.0)
        often = [jnp.concatenate([times[:, h * HALF:(h + 1) * HALF]] * 8, axis=0) for h in range(2)]
        blank = jnp.concatenate([blank] * 8, axis=0)
        new_row = lax.broadcasted_iota(jnp.int32, (8 * 16, 16), 0)
        new_col = lax.broadcasted_iota(jnp.int32, (8 * 16, 16), 1)
        fresh = ((lax.rem(new_row, 16) // STEPS == new_col // STEPS)
                 & (lax.rem(new_col, STEPS) <= lax.rem(new_row, STEPS)))
        nt = (((1,), (1,)), ((), ()))

        def dot_nt(a, b):
            return lax.dot_general(a, b, nt, preferred_element_type=jnp.float32)

        def rows_of(ref):
            return jnp.concatenate([ref[r].astype(jnp.float32) for r in range(4)], axis=0).astype(
                jnp.bfloat16)

        dq_all, dk_all, dv_all = rows_of(dq_ref), rows_of(dk_ref), rows_of(dv_ref)
        for g in range(KVH):
            queries = jnp.concatenate(
                [dq_all[:, (g * 8 + h) * DH:(g * 8 + h + 1) * DH] for h in range(8)], axis=0)
            wide = jnp.dot(queries, spread, preferred_element_type=jnp.float32).astype(jnp.bfloat16)
            keys_in = jnp.concatenate([zk[g, 0], zk[g, 1]], axis=1)
            values_in = jnp.concatenate([zv[g, 0], zv[g, 1]], axis=0)
            cut = slice(g * DH, (g + 1) * DH)
            s = [dot_nt(wide[:, h * 256:(h + 1) * 256], keys_in) * SCALE2 for h in range(2)]
            s_new = dot_nt(queries, dk_all[:, cut]) * SCALE2
            top = jnp.maximum(jnp.max(jnp.where(fresh, s_new, NEG), axis=1, keepdims=True),
                              jnp.where(blank > 0, 0.0, NEG))
            for h in range(2):
                top = jnp.maximum(top, jnp.max(jnp.where(often[h] > 0, s[h], NEG), axis=1, keepdims=True))
            w_new = jnp.where(fresh, jnp.exp2(s_new - top), 0.0)
            total = jnp.sum(w_new, axis=1, keepdims=True)
            total += jnp.where(blank > 0, blank * jnp.exp2(jnp.minimum(-top, 0.0)), 0.0)
            blend = jnp.dot(w_new.astype(jnp.bfloat16), dv_all[:, cut], preferred_element_type=jnp.float32)
            for h in range(2):
                w = jnp.where(often[h] > 0, jnp.exp2(s[h] - top), 0.0) * often[h]
                total += jnp.sum(w, axis=1, keepdims=True)
                blend += dot_nt(w.astype(jnp.bfloat16), values_in[:, h * HALF:(h + 1) * HALF])
            done = blend / total
            for h in range(8):
                for r in range(4):
                    dec_ref[r, :, (g * 8 + h) * DH:(g * 8 + h + 1) * DH] = done[
                        h * 16 + r * 4:h * 16 + r * 4 + 4].astype(jnp.bfloat16)

    def turn(tau, done):
        finishing = tau >= SPLIT
        pl.when(tau == SPLIT)(decode)
        for turn_of, since, number, event in events:
            pl.when((tau == turn_of) & (done[since] <= number))(event)
        for k, (pair, ky) in enumerate(order):
            @pl.when(tau == min(k, SPLIT))
            def _(pair=pair, ky=ky):
                arrived(pair, ky)

        @pl.when(tau < SPLIT)
        def _():
            note_keys(place_at(tau))

        @pl.when(tau == SPLIT)
        def _():
            lax.fori_loop(SPLIT, len(order), lambda k, c: (note_keys(place_at(k)), c)[1], 0)

        at_now = place_at(tau)
        own_count = jnp.where(at_now <= cb, mine, 0)
        here = jnp.where(tau == 0, jnp.minimum(guests, EARLY), guests)
        count = own_count + jnp.where(at_now <= mirror // 2, here, 0)
        guest_pairs = (guests + 1) // 2
        number = tau - SPLIT
        end_guest = number < guest_pairs
        first = 2 * jnp.where(end_guest, number, number - guest_pairs)
        remain = len(order) - SPLIT
        late_guests = end_guest & (first >= EARLY)
        steps = jnp.where(finishing, remain + jnp.where(late_guests, 1, 0), (count + 1) // 2)
        limit = jnp.where(finishing, jnp.where(end_guest, guests, mine), count)

        def tile_at(index):
            guest = jnp.where(finishing, end_guest, index >= own_count)
            v = jnp.where(finishing, index, index - own_count)
            own = index
            return (guest, v, jnp.where(guest, TILES + v, own),
                    jnp.where(guest, TILES - 1 - v, own) // 2, jnp.where(guest, mirror, blk))

        def item(i, carry):
            for turn_of, since, at_item, event in events:
                pl.when((tau >= since) & (tau < turn_of) & (done[since] + i == at_item))(event)
            at = place_at(jnp.where(finishing, lax.rem(SPLIT + i, len(order)), tau))
            index = jnp.where(finishing, first, 2 * i)
            lone = index + 1 >= limit
            guest, v_0, u_0, t, block = tile_at(index)
            _, v_1, u_1, _, _ = tile_at(index + 1)
            for v, here in ((v_0, True), (v_1, jnp.logical_not(lone))):
                @pl.when(here & guest & (tau == jnp.where(v >= EARLY, 1, 0)))
                def _(v=v):
                    take_guest(v)

            @pl.when(jnp.logical_not(lone))
            def _():
                tile_turn([u_0, u_1], t, block, at)

            @pl.when(lone)
            def _():
                tile_turn([u_0], t, block, at)
            return carry

        lax.fori_loop(0, steps, item, 0)

        @pl.when(finishing)
        def _():
            def end(k, c):
                guest, v, u, _, _ = tile_at(first + k)
                result(u)
                for h in range(2):
                    pl.when(guest)(lambda h=h: o_copy(v, h).start())
                    pl.when(jnp.logical_not(guest))(lambda h=h: own_out(u, h).start())
                return c
            lax.fori_loop(0, jnp.minimum(limit - first, 2), end, 0)
        return (done[0] + jnp.where(finishing, 0, steps),
                done[1] + jnp.where(finishing | (tau == 0), 0, steps))

    lax.fori_loop(0, SPLIT + (guests + 1) // 2 + (mine + 1) // 2, turn, (0, 0))

    kk = jnp.broadcast_to(jnp.max(kmx[...], axis=0, keepdims=True), (16, DH)).astype(jnp.bfloat16)

    def reach(u, farthest):
        far_score = lax.dot_general(kk, jnp.abs(qst[u]), (((1,), (1,)), ((), ())),
                                    preferred_element_type=jnp.float32)
        return jnp.maximum(farthest, far_score)

    farthest = lax.fori_loop(0, TILES, reach, jnp.zeros((16, TILE), jnp.float32))
    bound_ref[0, 0] = jnp.max(farthest)

    for index in range(2):
        for d in range(1, Z):
            z_copy(index, d).wait_send()
    when_loop(sent_tiles, lambda v: q_copy(v).wait_send())
    keys.finish()
    values.finish()
    for at in range(N_BLK // 2):
        keep_copy(at, 0).wait()
        keep_copy(at, 1).wait()
    for h in range(2):
        when_loop(mine, lambda u, h=h: own_out(u, h).wait())
        when_loop(guests, lambda v, h=h: o_copy(v, h).wait_send())
        when_loop(sent_tiles, lambda v, h=h: o_copy(v, h).wait_recv())


def fused(*args):
    vmem = pl.BlockSpec(memory_space=pltpu.VMEM)
    smem = pl.BlockSpec(memory_space=pltpu.SMEM)
    anywhere = pl.BlockSpec(memory_space=pl.ANY)
    bf16, f32 = jnp.bfloat16, jnp.float32
    slots = TILES + GUESTS
    return pl.pallas_call(
        fused_kernel,
        out_shape=(
            jax.ShapeDtypeStruct((ROWS, 4 * DH), bf16),
            jax.ShapeDtypeStruct((4, STEPS, HQ * DH), bf16),
            jax.ShapeDtypeStruct((N_BLK, 2, HALF, DH), bf16),
            jax.ShapeDtypeStruct((N_BLK, 2, DH // 2, ROWS), bf16),
            jax.ShapeDtypeStruct((1, 1), f32),
        ),
        in_specs=[anywhere] + [vmem] * 6 + [smem] * 2,
        out_specs=(anywhere, vmem, anywhere, anywhere, smem),
        scratch_shapes=[
            pltpu.VMEM((ROWS, 4 * DH), bf16),
            pltpu.VMEM((N_BLK, 2, HALF, DH), bf16),
            pltpu.VMEM((N_BLK, 2, DH // 2, ROWS), bf16),
            pltpu.VMEM((N_BLK, 2, HALF, DH), bf16),
            pltpu.VMEM((Z, 2, HALF, DH), bf16),
            pltpu.VMEM((Z, 2, DH // 2, ROWS), bf16),
            pltpu.VMEM((slots, TILE, DH), bf16),
            pltpu.VMEM((slots, 144, TILE), f32),
            pltpu.VMEM((slots, 2, 256, DH), bf16),
            pltpu.VMEM((8, DH), f32),
            pltpu.SemaphoreType.DMA((2, COPIES)),
            pltpu.SemaphoreType.DMA((2, COPIES)),
            pltpu.SemaphoreType.DMA((GUESTS,)),
            pltpu.SemaphoreType.DMA((GUESTS,)),
            pltpu.SemaphoreType.DMA((GUESTS, 2)),
            pltpu.SemaphoreType.DMA((GUESTS, 2)),
            pltpu.SemaphoreType.DMA((2, Z)),
            pltpu.SemaphoreType.DMA((2, Z)),
            pltpu.SemaphoreType.DMA((19 + 2 * TILES,)),
        ],
        compiler_params=pltpu.CompilerParams(
            collective_id=0, has_side_effects=True, vmem_limit_bytes=56 << 20),
        cost_estimate=pl.CostEstimate(flops=2 * 10**10, bytes_accessed=2 * 10**7,
                                      transcendentals=4 * 10**7),
        name="prefill",
    )(*args)


def online_attend(queries, first_row, key_rows, value_rows):
    count, length = queries.shape[0], key_rows.shape[0]
    per_head = queries.shape[1] // DH
    grouped = queries.reshape(count, per_head, DH)
    positions = first_row + jnp.arange(count, dtype=jnp.int32)
    step_keys = 512

    def body(turn, state):
        top, total, blend = state
        at = turn * step_keys
        k = lax.dynamic_slice_in_dim(key_rows, at, step_keys, 0)
        v = lax.dynamic_slice_in_dim(value_rows, at, step_keys, 0)
        s = jnp.einsum("tgd,sd->gts", grouped, k, preferred_element_type=jnp.float32) * DH**-0.5
        visible = positions[:, None] >= at + jnp.arange(step_keys, dtype=jnp.int32)[None, :]
        s = jnp.where(visible, s, NEG)
        newest = jnp.maximum(top, jnp.max(s, axis=-1))
        weights = jnp.where(visible, jnp.exp(s - newest[..., None]), 0.0)
        fading = jnp.exp(top - newest)
        total = total * fading + jnp.sum(weights, axis=-1)
        update = jnp.einsum("gts,sd->tgd", weights.astype(jnp.bfloat16), v,
                            preferred_element_type=jnp.float32)
        return newest, total, blend * jnp.transpose(fading)[..., None] + update

    initial = (jnp.full((per_head, count), NEG, jnp.float32),
               jnp.zeros((per_head, count), jnp.float32),
               jnp.zeros((count, per_head, DH), jnp.float32))
    turns = (first_row + count) // step_keys
    _, total, blend = lax.fori_loop(0, turns, body, initial)
    return (blend / jnp.transpose(total)[..., None]).astype(jnp.bfloat16).reshape(queries.shape)


def on_device(pre_q, pre_k, pre_v, routes, dec_q, dec_k, dec_v, table, ctx_len):
    blk = lax.axis_index("blk")
    prefill_out, decode_out, k_all, v_all, bound = fused(
        pre_q, pre_k.T, pre_v.T, routes.T, dec_q, dec_k, dec_v, table, ctx_len)

    def slow(prefill_out, k_all, v_all, pre_q):
        v = v_all.reshape(N_BLK, DH, ROWS).transpose(0, 2, 1)
        return online_attend(pre_q, blk * ROWS, k_all.reshape(N_BLK * ROWS, DH),
                             v.reshape(N_BLK * ROWS, DH))

    safe = bound[0, 0] * SCALE2 <= SAFE
    prefill_out = lax.cond(safe, lambda done, *unused: done, slow,
                           prefill_out, k_all, v_all, pre_q)
    return prefill_out, decode_out


def solution(mesh):
    in_specs = (
        P("blk", "pool"),
        P("blk", "pool"),
        P("blk", "pool"),
        P("blk", None),
        P(("blk", "pool"), None, None),
        P(("blk", "pool"), None, None),
        P(("blk", "pool"), None, None),
        P(("blk", "pool"), None),
        P(("blk", "pool")),
    )
    out_specs = (P("blk", "pool"), P(("blk", "pool"), None, None))
    return jax.shard_map(
        on_device, mesh=mesh, in_specs=in_specs, out_specs=out_specs, check_vma=False
    )
```

```python
import functools

import jax
import jax.numpy as jnp
from jax import lax
from jax.experimental import pallas as pl
from jax.experimental.pallas import tpu as pltpu
from jax.sharding import PartitionSpec as P

HQ = 32
KVH = 4
DH = 128
PAGE = 16
STEPS = 4
PPR = 8

N_BLK = 16
N_POOL = 8
Z = 4
ROWS = 1024
HALF = ROWS // 2
TILE = 512
TILES = 8
GUESTS = 4
SCALE2 = DH**-0.5 * 1.4426950408889634
SPLIT = 7
EARLY = 4
SAFE = 100.0
NEG = -1e30
MESH = pl.DeviceIdType.MESH

A1, A2, B1, B2, SIB, COPIES = 0, 2, 4, 12, 20, 36


def fused_kernel(q_ref, k_ref, v_ref, routes_ref, dq_ref, dk_ref, dv_ref, table_ref, ctx_ref,
                 out_ref, dec_ref, kall_ref, vall_ref, bound_ref,
                 qin, kbuf, vbuf, kun, zk, zv, qst, acc, ostage, kmx,
                 send, recv, qsend, qrecv, osend, orecv, zsend, zrecv, local):
    blk, pool = lax.axis_index("blk"), lax.axis_index("pool")
    core = lax.rem(blk, 2)
    cb = blk // 2
    x_hi, y = cb // 4, lax.rem(cb, 4)
    z, x_lo = pool // 2, lax.rem(pool, 2)
    mirror = N_BLK - 1 - blk

    def block_of(xh, yy):
        return (xh * 4 + yy) * 2 + core

    def along_x(k):
        return ((x_hi, x_lo), (x_hi, 1 - x_lo), (1 - x_hi, 1 - x_lo), (1 - x_hi, x_lo))[k]

    def along_y(k):
        return lax.rem(y + (0, 1, 3, 2)[k], 4)

    def device(kx, ky):
        xh, xl = along_x(kx)
        return (block_of(xh, along_y(ky)), z * 2 + xl)

    def at_z(d):
        return (blk, lax.rem(z + d, Z) * 2 + x_lo)

    sibling = (blk + 1 - 2 * core, pool)
    partner = (mirror, z * 2 + 1 - x_lo)

    barrier = pltpu.get_barrier_semaphore()
    peers = [device(1, 0), device(2, 0), device(0, 1), device(0, 2), sibling, partner]
    peers += [at_z(d) for d in range(1, Z)]
    for peer in peers:
        pl.semaphore_signal(barrier, inc=1, device_id=peer, device_id_type=MESH)
    q_in = pltpu.make_async_copy(q_ref, qin, local.at[0])
    q_in.start()

    kbuf[blk, x_lo] = jnp.concatenate([k_ref[:, :HALF], k_ref[:, HALF:]], axis=0).T
    vbuf[blk, x_lo] = v_ref[...]
    pl.semaphore_wait(barrier, len(peers))

    class Gather:
        def __init__(self, index, buf, rows, x_first):
            self.index, self.buf, self.rows, self.x_first = index, buf, rows, x_first

        def place(self, ka, kb):
            return (ka, kb) if self.x_first else (kb, ka)

        def piece(self, ka, kb, half=None):
            kx, ky = self.place(ka, kb)
            xh, xl = along_x(kx)
            whole = self.buf.at[block_of(xh, along_y(ky)), xl]
            if half is None:
                return whole
            return whole.at[pl.ds(half * self.rows // 2, self.rows // 2)]

        def copy(self, slot, ka, kb, half, to, there=None):
            there = slot if there is None else there
            ref = self.piece(ka, kb, half)
            return pltpu.make_async_remote_copy(
                src_ref=ref, dst_ref=ref,
                send_sem=send.at[self.index, slot], recv_sem=recv.at[self.index, there],
                device_id=to, device_id_type=MESH)

        def neighbour(self, axis, n):
            ka, kb = ((n + 1, 0), (0, n + 1))[axis]
            return device(*self.place(ka, kb))

        def seen(self, axis, n):
            is_x = (axis == 0) == self.x_first
            return n if is_x else 1 - n

        def all_copies(self):
            out = {}
            for n in range(2):
                out["a1", n] = lambda n=n: self.copy(
                    A1 + n, 0, 0, None, self.neighbour(0, n), A1 + self.seen(0, n))
                out["a2", n] = lambda n=n: self.copy(
                    A2 + n, 2 - n, 0, n, self.neighbour(0, n))
                for ka in range(4):
                    out["b1", ka, n] = lambda n=n, ka=ka: self.copy(
                        B1 + ka * 2 + n, ka, 0, None, self.neighbour(1, n),
                        B1 + ka * 2 + self.seen(1, n))
                    out["b2", ka, n] = lambda n=n, ka=ka: self.copy(
                        B2 + ka * 2 + n, ka, 2 - n, n, self.neighbour(1, n))
            for ka in range(4):
                for kb in range(4):
                    out["sib", ka, kb] = lambda ka=ka, kb=kb: self.copy(
                        SIB + ka * 4 + kb, ka, kb, None, sibling)
            return out

        def start(self, *key):
            self.all_copies()[key]().start()

        def arrive(self, slot, ka, kb, half=None):
            ref = self.piece(ka, kb, half)
            pltpu.make_async_remote_copy(
                src_ref=ref, dst_ref=ref, send_sem=send.at[self.index, slot],
                recv_sem=recv.at[self.index, slot], device_id=sibling,
                device_id_type=MESH).wait_recv()

        def got_a1(self, n):
            self.arrive(A1 + n, n + 1, 0)
            self.start("a2", 1 - n)
            self.start("sib", n + 1, 0)

        def pass_b1(self, ka):
            self.start("b1", ka, 0)
            self.start("b1", ka, 1)

        def got_a2(self):
            for half in range(2):
                self.arrive(A2 + half, 3, 0, half)
            self.start("sib", 3, 0)
            self.pass_b1(3)

        def got_b1(self, ka, n):
            self.arrive(B1 + ka * 2 + n, ka, n + 1)
            self.start("b2", ka, 1 - n)
            self.start("sib", ka, n + 1)

        def got_b2(self, ka):
            for half in range(2):
                self.arrive(B2 + ka * 2 + half, ka, 3, half)
            self.start("sib", ka, 3)

        def got_sib(self, ka, kb):
            kx, ky = self.place(ka, kb)
            xh, xl = along_x(kx)
            there = (xh * 4 + along_y(ky)) * 2 + 1 - core
            ref = self.buf.at[there, xl]
            slot = SIB + ka * 4 + kb
            pltpu.make_async_remote_copy(
                src_ref=ref, dst_ref=ref, send_sem=send.at[self.index, slot],
                recv_sem=recv.at[self.index, slot], device_id=sibling,
                device_id_type=MESH).wait_recv()

        def sib_xy(self, kx, ky):
            self.got_sib(*((kx, ky) if self.x_first else (ky, kx)))

        def finish(self):
            for make in self.all_copies().values():
                make().wait_send()

    keys = Gather(0, kbuf, HALF, True)
    values = Gather(1, vbuf, DH // 2, False)

    keys.start("a1", 0)
    values.start("b1", 0, 0)
    keys.start("sib", 0, 0)
    values.start("sib", 0, 0)
    keys.start("a1", 1)
    values.start("b1", 0, 1)
    for n in range(2):
        values.start("a1", n)
        keys.start("b1", 0, n)

    high = blk >= N_BLK // 2
    giver = jnp.where(high, blk, mirror)
    moved = jnp.where(giver >= 14, 3, jnp.where(giver >= 10, 2, 1))
    mine = jnp.where(high, TILES - moved, TILES)
    guests = jnp.where(high, 0, moved)
    sent_tiles = jnp.where(high, moved, 0)

    def q_copy(v):
        return pltpu.make_async_remote_copy(
            src_ref=qst.at[TILES - 1 - v], dst_ref=qst.at[TILES + v],
            send_sem=qsend.at[v], recv_sem=qrecv.at[v],
            device_id=partner, device_id_type=MESH)

    def out_part(u, h):
        row = pl.multiple_of(u // 2 * 256, 256)
        column = pl.multiple_of((lax.rem(u, 2) * 2 + h) * DH, DH)
        return out_ref.at[pl.ds(row, 256), pl.ds(column, DH)]

    def o_copy(v, h):
        return pltpu.make_async_remote_copy(
            src_ref=ostage.at[TILES + v, h], dst_ref=out_part(TILES - 1 - v, h),
            send_sem=osend.at[v, h], recv_sem=orecv.at[v, h],
            device_id=partner, device_id_type=MESH)

    def when_loop(count, body):
        def step(v, carry):
            body(v)
            return carry
        lax.fori_loop(0, count, step, 0)

    def z_copy(index, d):
        buf, there = ((kbuf, zk), (vbuf, zv))[index]
        return pltpu.make_async_remote_copy(
            src_ref=buf.at[blk], dst_ref=there.at[z],
            send_sem=zsend.at[index, d], recv_sem=zrecv.at[index, d],
            device_id=at_z(d), device_id_type=MESH)

    def z_arrive(index, d):
        ref = (zk, zv)[index].at[lax.rem(z + Z - d, Z)]
        pltpu.make_async_remote_copy(
            src_ref=ref, dst_ref=ref, send_sem=zsend.at[index, d], recv_sem=zrecv.at[index, d],
            device_id=sibling, device_id_type=MESH).wait_recv()

    def z_own(index):
        buf, there = ((kbuf, zk), (vbuf, zv))[index]
        return pltpu.make_async_copy(buf.at[blk], there.at[z], local.at[1 + index])

    d_in = lax.broadcasted_iota(jnp.int32, (DH, 4 * DH), 0)
    column = lax.broadcasted_iota(jnp.int32, (DH, 4 * DH), 1)
    half, lane = column // 256, lax.rem(column, 256)
    source = lax.rem(lane, 128) - 64 * half
    spread = jnp.where((source >= 0) & (source < 64) & (source + (lane // 128) * 64 == d_in),
                       1.0, 0.0).astype(jnp.bfloat16)

    def clear(u):
        acc[u] = jnp.zeros((144, TILE), jnp.float32)

    q_in.wait()
    for u in range(TILES):
        t, hp = u // 2, u % 2
        for h in range(2):
            col = (hp * 2 + h) * DH
            qst[u, h * 256:(h + 1) * 256, :] = qin[t * 256:(t + 1) * 256, col:col + DH]
    when_loop(TILES + GUESTS, clear)
    kmx[...] = jnp.zeros_like(kmx)

    ones = jnp.ones((16, HALF), jnp.bfloat16)

    def scores(u, block, h):
        return lax.dot_general(kun[block, h], qst[u], (((1,), (1,)), ((), ())),
                               preferred_element_type=jnp.float32)

    def mixed(s, block, h, visible=None):
        weights = jnp.exp2(s * SCALE2)
        if visible is not None:
            weights = jnp.where(visible, weights, 0.0)
        cut = slice(h * HALF, (h + 1) * HALF)
        values_in = jnp.concatenate([vbuf[block, 0, :, cut], vbuf[block, 1, :, cut], ones], axis=0)
        return jnp.dot(values_in, weights.astype(jnp.bfloat16), preferred_element_type=jnp.float32)

    def full(tiles, chunks):
        work = [(u, chunk) for u in tiles for chunk in chunks]
        ahead = scores(work[0][0], *work[0][1])
        total = None
        for i, (u, chunk) in enumerate(work):
            now = ahead
            if i + 1 < len(work):
                ahead = scores(work[i + 1][0], *work[i + 1][1])
            part = mixed(now, *chunk)
            total = part if i % len(chunks) == 0 else total + part
            if i % len(chunks) == len(chunks) - 1:
                acc[u] += total

    def chunks_of(at):
        return [(2 * at + core_at, h) for core_at in range(2) for h in range(2)]

    def diagonal(tiles, t, block):
        key_at = lax.broadcasted_iota(jnp.int32, (HALF, TILE), 0)
        row_at = lax.rem(lax.broadcasted_iota(jnp.int32, (HALF, TILE), 1), 256)
        late = t // 2
        visible = key_at <= row_at + (t - 2 * late) * 256

        @pl.when(late == 0)
        def _():
            ahead = [scores(u, block, 0) for u in tiles]
            for u, s in zip(tiles, ahead):
                acc[u] += mixed(s, block, 0, visible)

        @pl.when(late == 1)
        def _():
            ahead = [scores(u, block, h) for u in tiles for h in range(2)]
            for i, u in enumerate(tiles):
                acc[u] += (mixed(ahead[2 * i], block, 0)
                           + mixed(ahead[2 * i + 1], block, 1, visible))

    def tile_turn(tiles, t, tile_block, at):
        tile_cb = tile_block // 2

        @pl.when(at < tile_cb)
        def _():
            full(tiles, chunks_of(at))

        @pl.when(at == tile_cb)
        def _():
            @pl.when(lax.rem(tile_block, 2) == 1)
            def _():
                full(tiles, [(2 * at, 0), (2 * at, 1)])
            diagonal(tiles, t, tile_block)

    def keep_copy(at, slot):
        ref, buf = ((kall_ref, kun), (vall_ref, vbuf))[slot]
        return pltpu.make_async_copy(buf.at[pl.ds(2 * at, 2)], ref.at[pl.ds(2 * at, 2)],
                                     local.at[3 + slot + 2 * at])

    def note_keys(at):
        for core_at in range(2):
            for xl in range(2):
                piece = jnp.concatenate(
                    [kbuf[2 * at + core_at, p, :, xl * 64:(xl + 1) * 64] for p in range(2)], axis=1)
                kun[2 * at + core_at, xl] = piece
                size = jnp.abs(piece.astype(jnp.float32)).reshape(HALF // 8, 8, DH)
                kmx[...] = jnp.maximum(kmx[...], jnp.max(size, axis=0))
        keep_copy(at, 0).start()
        keep_copy(at, 1).start()

    def take_guest(v):
        q_copy(v).wait_recv()

    def z_start():
        for index in range(2):
            z_own(index).start()
            for d in range(1, Z):
                z_copy(index, d).start()

    def both(method, *keys_of):
        for args in keys_of:
            for gather in (keys, values):
                getattr(gather, method)(*args)

    near, far = (0, 1), (2, 3)
    order = [(near, 0), (far, 0), (near, 1), (near, 2), (far, 1), (far, 2), (near, 3), (far, 3)]
    places = [along_x(pair[0])[0] * 4 + along_y(ky) for pair, ky in order]

    events = [
        (1, 0, 1, z_start),
        (1, 0, 1, lambda: both("got_a2", ())),
        (1, 0, 4, lambda: both("got_b1", (1, 0), (1, 1))),
        (1, 0, 99, lambda: both("got_b2", (0,))),
        (3, 1, 1, lambda: both("got_b1", (2, 0), (2, 1))),
        (4, 1, 4, lambda: both("got_b1", (3, 0), (3, 1))),
        (4, 1, 5, lambda: both("got_b2", (1,), (2,))),
        (SPLIT, 1, 8, lambda: both("got_b2", (3,))),
    ]

    keys.got_a1(0)
    keys.pass_b1(1)
    values.got_a1(0)
    values.pass_b1(1)
    values.got_a1(1)
    keys.got_a1(1)
    values.got_b1(0, 0)
    keys.got_b1(0, 0)
    keys.got_b1(0, 1)
    values.got_b1(0, 1)
    keys.pass_b1(2)
    values.pass_b1(2)

    when_loop(sent_tiles, lambda v: q_copy(v).start())

    def result(u):
        total = acc[u]
        ostage[u] = (total[:DH] / total[DH:DH + 1]).T.astype(jnp.bfloat16).reshape(2, 256, DH)

    def own_out(u, h):
        return pltpu.make_async_copy(ostage.at[u, h], out_part(u, h), local.at[19 + 2 * u + h])

    def place_at(tau):
        at = places[0]
        for k in range(1, len(places)):
            at = jnp.where(tau == k, places[k], at)
        return at

    def arrived(pair, ky):
        for kx in pair:
            keys.sib_xy(kx, ky)
            values.sib_xy(kx, ky)

    def decode():
        for index in range(2):
            z_own(index).wait()
            for d in range(1, Z):
                z_arrive(index, d)
        owned = (jnp.broadcast_to(routes_ref[...], (16, 64)) == pool).astype(jnp.float32)
        page_at = lax.broadcasted_iota(jnp.int32, (64, ROWS), 0)
        token_page = lax.broadcasted_iota(jnp.int32, (64, ROWS), 1) // PAGE
        pick = owned.astype(jnp.bfloat16)
        rank = jnp.dot(pick, (page_at < token_page).astype(jnp.float32).astype(jnp.bfloat16),
                       preferred_element_type=jnp.float32)
        held = jnp.dot(pick, (page_at == token_page).astype(jnp.float32).astype(jnp.bfloat16),
                       preferred_element_type=jnp.float32)
        slot = jnp.where(held > 0, rank, -1.0)
        filled = jnp.sum(owned, axis=1, keepdims=True)
        row_of = lax.broadcasted_iota(jnp.int32, (16, ROWS), 0) // STEPS
        in_page = lax.rem(lax.broadcasted_iota(jnp.int32, (16, ROWS), 1), PAGE)

        def by_row(values_of):
            out = jnp.full((16, ROWS), values_of[0], jnp.int32)
            for r in range(1, 4):
                out = jnp.where(row_of == r, values_of[r], out)
            return out

        allowed = by_row([ctx_ref[r] for r in range(4)])
        times = jnp.zeros((16, ROWS), jnp.float32)
        blank = jnp.zeros((16, 1), jnp.float32)
        for p in range(PPR):
            named = by_row([table_ref[r, p] for r in range(4)]).astype(jnp.float32)
            times += jnp.where((named == slot) & (p * PAGE + in_page < allowed), 1.0, 0.0)
            shown = jnp.clip(allowed[:, :1] - p * PAGE, 0, PAGE).astype(jnp.float32)
            blank += jnp.where(named[:, :1] >= filled, shown, 0.0)
        often = [jnp.concatenate([times[:, h * HALF:(h + 1) * HALF]] * 8, axis=0) for h in range(2)]
        blank = jnp.concatenate([blank] * 8, axis=0)
        new_row = lax.broadcasted_iota(jnp.int32, (8 * 16, 16), 0)
        new_col = lax.broadcasted_iota(jnp.int32, (8 * 16, 16), 1)
        fresh = ((lax.rem(new_row, 16) // STEPS == new_col // STEPS)
                 & (lax.rem(new_col, STEPS) <= lax.rem(new_row, STEPS)))
        nt = (((1,), (1,)), ((), ()))

        def dot_nt(a, b):
            return lax.dot_general(a, b, nt, preferred_element_type=jnp.float32)

        def rows_of(ref):
            return jnp.concatenate([ref[r].astype(jnp.float32) for r in range(4)], axis=0).astype(
                jnp.bfloat16)

        dq_all, dk_all, dv_all = rows_of(dq_ref), rows_of(dk_ref), rows_of(dv_ref)
        for g in range(KVH):
            queries = jnp.concatenate(
                [dq_all[:, (g * 8 + h) * DH:(g * 8 + h + 1) * DH] for h in range(8)], axis=0)
            wide = jnp.dot(queries, spread, preferred_element_type=jnp.float32).astype(jnp.bfloat16)
            keys_in = jnp.concatenate([zk[g, 0], zk[g, 1]], axis=1)
            values_in = jnp.concatenate([zv[g, 0], zv[g, 1]], axis=0)
            cut = slice(g * DH, (g + 1) * DH)
            s = [dot_nt(wide[:, h * 256:(h + 1) * 256], keys_in) * SCALE2 for h in range(2)]
            s_new = dot_nt(queries, dk_all[:, cut]) * SCALE2
            top = jnp.maximum(jnp.max(jnp.where(fresh, s_new, NEG), axis=1, keepdims=True),
                              jnp.where(blank > 0, 0.0, NEG))
            for h in range(2):
                top = jnp.maximum(top, jnp.max(jnp.where(often[h] > 0, s[h], NEG), axis=1, keepdims=True))
            w_new = jnp.where(fresh, jnp.exp2(s_new - top), 0.0)
            total = jnp.sum(w_new, axis=1, keepdims=True)
            total += jnp.where(blank > 0, blank * jnp.exp2(jnp.minimum(-top, 0.0)), 0.0)
            blend = jnp.dot(w_new.astype(jnp.bfloat16), dv_all[:, cut], preferred_element_type=jnp.float32)
            for h in range(2):
                w = jnp.where(often[h] > 0, jnp.exp2(s[h] - top), 0.0) * often[h]
                total += jnp.sum(w, axis=1, keepdims=True)
                blend += dot_nt(w.astype(jnp.bfloat16), values_in[:, h * HALF:(h + 1) * HALF])
            done = blend / total
            for h in range(8):
                for r in range(4):
                    dec_ref[r, :, (g * 8 + h) * DH:(g * 8 + h + 1) * DH] = done[
                        h * 16 + r * 4:h * 16 + r * 4 + 4].astype(jnp.bfloat16)

    def turn(tau, done):
        finishing = tau >= SPLIT
        pl.when(tau == SPLIT)(decode)
        for turn_of, since, number, event in events:
            pl.when((tau == turn_of) & (done[since] <= number))(event)
        for k, (pair, ky) in enumerate(order):
            @pl.when(tau == min(k, SPLIT))
            def _(pair=pair, ky=ky):
                arrived(pair, ky)

        @pl.when(tau < SPLIT)
        def _():
            note_keys(place_at(tau))

        @pl.when(tau == SPLIT)
        def _():
            lax.fori_loop(SPLIT, len(order), lambda k, c: (note_keys(place_at(k)), c)[1], 0)

        at_now = place_at(tau)
        own_count = jnp.where(at_now <= cb, mine, 0)
        here = jnp.where(tau == 0, jnp.minimum(guests, EARLY), guests)
        count = own_count + jnp.where(at_now <= mirror // 2, here, 0)
        guest_pairs = (guests + 1) // 2
        number = tau - SPLIT
        end_guest = number < guest_pairs
        first = 2 * jnp.where(end_guest, number, number - guest_pairs)
        remain = len(order) - SPLIT
        late_guests = end_guest & (first >= EARLY)
        steps = jnp.where(finishing, remain + jnp.where(late_guests, 1, 0), (count + 1) // 2)
        limit = jnp.where(finishing, jnp.where(end_guest, guests, mine), count)

        def tile_at(index):
            guest = jnp.where(finishing, end_guest, index >= own_count)
            v = jnp.where(finishing, index, index - own_count)
            own = index
            return (guest, v, jnp.where(guest, TILES + v, own),
                    jnp.where(guest, TILES - 1 - v, own) // 2, jnp.where(guest, mirror, blk))

        def item(i, carry):
            for turn_of, since, at_item, event in events:
                pl.when((tau >= since) & (tau < turn_of) & (done[since] + i == at_item))(event)
            at = place_at(jnp.where(finishing, lax.rem(SPLIT + i, len(order)), tau))
            index = jnp.where(finishing, first, 2 * i)
            lone = index + 1 >= limit
            guest, v_0, u_0, t, block = tile_at(index)
            _, v_1, u_1, _, _ = tile_at(index + 1)
            for v, here in ((v_0, True), (v_1, jnp.logical_not(lone))):
                @pl.when(here & guest & (tau == jnp.where(v >= EARLY, 1, 0)))
                def _(v=v):
                    take_guest(v)

            @pl.when(jnp.logical_not(lone))
            def _():
                tile_turn([u_0, u_1], t, block, at)

            @pl.when(lone)
            def _():
                tile_turn([u_0], t, block, at)
            return carry

        lax.fori_loop(0, steps, item, 0)

        @pl.when(finishing)
        def _():
            def end(k, c):
                guest, v, u, _, _ = tile_at(first + k)
                result(u)
                for h in range(2):
                    pl.when(guest)(lambda h=h: o_copy(v, h).start())
                    pl.when(jnp.logical_not(guest))(lambda h=h: own_out(u, h).start())
                return c
            lax.fori_loop(0, jnp.minimum(limit - first, 2), end, 0)
        return (done[0] + jnp.where(finishing, 0, steps),
                done[1] + jnp.where(finishing | (tau == 0), 0, steps))

    lax.fori_loop(0, SPLIT + (guests + 1) // 2 + (mine + 1) // 2, turn, (0, 0))

    kk = jnp.broadcast_to(jnp.max(kmx[...], axis=0, keepdims=True), (16, DH)).astype(jnp.bfloat16)

    def reach(u, farthest):
        far_score = lax.dot_general(kk, jnp.abs(qst[u]), (((1,), (1,)), ((), ())),
                                    preferred_element_type=jnp.float32)
        return jnp.maximum(farthest, far_score)

    farthest = lax.fori_loop(0, TILES, reach, jnp.zeros((16, TILE), jnp.float32))
    bound_ref[0, 0] = jnp.max(farthest)

    for index in range(2):
        for d in range(1, Z):
            z_copy(index, d).wait_send()
    when_loop(sent_tiles, lambda v: q_copy(v).wait_send())
    keys.finish()
    values.finish()
    for at in range(N_BLK // 2):
        keep_copy(at, 0).wait()
        keep_copy(at, 1).wait()
    for h in range(2):
        when_loop(mine, lambda u, h=h: own_out(u, h).wait())
        when_loop(guests, lambda v, h=h: o_copy(v, h).wait_send())
        when_loop(sent_tiles, lambda v, h=h: o_copy(v, h).wait_recv())


def fused(*args):
    vmem = pl.BlockSpec(memory_space=pltpu.VMEM)
    smem = pl.BlockSpec(memory_space=pltpu.SMEM)
    anywhere = pl.BlockSpec(memory_space=pl.ANY)
    bf16, f32 = jnp.bfloat16, jnp.float32
    slots = TILES + GUESTS
    return pl.pallas_call(
        fused_kernel,
        out_shape=(
            jax.ShapeDtypeStruct((ROWS, 4 * DH), bf16),
            jax.ShapeDtypeStruct((4, STEPS, HQ * DH), bf16),
            jax.ShapeDtypeStruct((N_BLK, 2, HALF, DH), bf16),
            jax.ShapeDtypeStruct((N_BLK, 2, DH // 2, ROWS), bf16),
            jax.ShapeDtypeStruct((1, 1), f32),
        ),
        in_specs=[anywhere] + [vmem] * 6 + [smem] * 2,
        out_specs=(anywhere, vmem, anywhere, anywhere, smem),
        scratch_shapes=[
            pltpu.VMEM((ROWS, 4 * DH), bf16),
            pltpu.VMEM((N_BLK, 2, HALF, DH), bf16),
            pltpu.VMEM((N_BLK, 2, DH // 2, ROWS), bf16),
            pltpu.VMEM((N_BLK, 2, HALF, DH), bf16),
            pltpu.VMEM((Z, 2, HALF, DH), bf16),
            pltpu.VMEM((Z, 2, DH // 2, ROWS), bf16),
            pltpu.VMEM((slots, TILE, DH), bf16),
            pltpu.VMEM((slots, 144, TILE), f32),
            pltpu.VMEM((slots, 2, 256, DH), bf16),
            pltpu.VMEM((8, DH), f32),
            pltpu.SemaphoreType.DMA((2, COPIES)),
            pltpu.SemaphoreType.DMA((2, COPIES)),
            pltpu.SemaphoreType.DMA((GUESTS,)),
            pltpu.SemaphoreType.DMA((GUESTS,)),
            pltpu.SemaphoreType.DMA((GUESTS, 2)),
            pltpu.SemaphoreType.DMA((GUESTS, 2)),
            pltpu.SemaphoreType.DMA((2, Z)),
            pltpu.SemaphoreType.DMA((2, Z)),
            pltpu.SemaphoreType.DMA((19 + 2 * TILES,)),
        ],
        compiler_params=pltpu.CompilerParams(
            collective_id=0, has_side_effects=True, vmem_limit_bytes=56 << 20),
        cost_estimate=pl.CostEstimate(flops=2 * 10**10, bytes_accessed=2 * 10**7,
                                      transcendentals=4 * 10**7),
        name="prefill",
    )(*args)


def online_attend(queries, first_row, key_rows, value_rows):
    count, length = queries.shape[0], key_rows.shape[0]
    per_head = queries.shape[1] // DH
    grouped = queries.reshape(count, per_head, DH)
    positions = first_row + jnp.arange(count, dtype=jnp.int32)
    step_keys = 512

    def body(turn, state):
        top, total, blend = state
        at = turn * step_keys
        k = lax.dynamic_slice_in_dim(key_rows, at, step_keys, 0)
        v = lax.dynamic_slice_in_dim(value_rows, at, step_keys, 0)
        s = jnp.einsum("tgd,sd->gts", grouped, k, preferred_element_type=jnp.float32) * DH**-0.5
        visible = positions[:, None] >= at + jnp.arange(step_keys, dtype=jnp.int32)[None, :]
        s = jnp.where(visible, s, NEG)
        newest = jnp.maximum(top, jnp.max(s, axis=-1))
        weights = jnp.where(visible, jnp.exp(s - newest[..., None]), 0.0)
        fading = jnp.exp(top - newest)
        total = total * fading + jnp.sum(weights, axis=-1)
        update = jnp.einsum("gts,sd->tgd", weights.astype(jnp.bfloat16), v,
                            preferred_element_type=jnp.float32)
        return newest, total, blend * jnp.transpose(fading)[..., None] + update

    initial = (jnp.full((per_head, count), NEG, jnp.float32),
               jnp.zeros((per_head, count), jnp.float32),
               jnp.zeros((count, per_head, DH), jnp.float32))
    turns = (first_row + count) // step_keys
    _, total, blend = lax.fori_loop(0, turns, body, initial)
    return (blend / jnp.transpose(total)[..., None]).astype(jnp.bfloat16).reshape(queries.shape)


def on_device(pre_q, pre_k, pre_v, routes, dec_q, dec_k, dec_v, table, ctx_len):
    blk = lax.axis_index("blk")
    prefill_out, decode_out, k_all, v_all, bound = fused(
        pre_q, pre_k.T, pre_v.T, routes.T, dec_q, dec_k, dec_v, table, ctx_len)

    def slow(prefill_out, k_all, v_all, pre_q):
        v = v_all.reshape(N_BLK, DH, ROWS).transpose(0, 2, 1)
        return online_attend(pre_q, blk * ROWS, k_all.reshape(N_BLK * ROWS, DH),
                             v.reshape(N_BLK * ROWS, DH))

    safe = bound[0, 0] * SCALE2 <= SAFE
    prefill_out = lax.cond(safe, lambda done, *unused: done, slow,
                           prefill_out, k_all, v_all, pre_q)
    return prefill_out, decode_out


def solution(mesh):
    in_specs = (
        P("blk", "pool"),
        P("blk", "pool"),
        P("blk", "pool"),
        P("blk", None),
        P(("blk", "pool"), None, None),
        P(("blk", "pool"), None, None),
        P(("blk", "pool"), None, None),
        P(("blk", "pool"), None),
        P(("blk", "pool")),
    )
    out_specs = (P("blk", "pool"), P(("blk", "pool"), None, None))
    return jax.shard_map(
        on_device, mesh=mesh, in_specs=in_specs, out_specs=out_specs, check_vma=False
    )
```
